32 devices in a mesh: group: 4 (over z), tok: 8 (over y, x, core).
Axes of the slice: x: 2, y: 2, z: 4, core: 2. Of those that a mesh axis runs over, the one named last changes fastest.
Arguments:
- tokens: bfloat16 [2048, 1792], P(('group', 'tok')), may hold values from -6 to 6
- norm_gains: float32 [2, 1792], replicated, may hold values from 0.25 to 1.75
- qk_weight: bfloat16 [2, 256, 1792], replicated, may hold values from -0.125 to 0.125
- mixer_weight: bfloat16 [3, 1792, 1792], P(None, 'tok'), may hold values from -0.125 to 0.125
- conv_weight: float32 [3, 1792], P(None, 'tok'), may hold values from -1 to 1
- out_weight: bfloat16 [2, 1792, 1792], P(None, 'tok'), may hold values from -0.09375 to 0.09375
- ffn_weight: bfloat16 [2, 4864, 1792], P(None, 'tok'), may hold values from -0.125 to 0.125
- down_weight: bfloat16 [4864, 1792], P('tok'), may hold values from -0.078125 to 0.078125
- cached_states: float32 [32, 273, 1792], P('group', None, 'tok'), may hold values from -8 to 8
- cached_norms: float32 [32, 273, 16], P('group'), as said below
- conv_cache: bfloat16 [32, 2, 1792], P('group', None, 'tok'), may hold values from -6 to 6
- cached_lengths: int32 [32], P('group'), may hold values from 0 to 31744
- new_lengths: int32 [4, 8], P('group'), may hold values from 1 to 504, as said below
- state_source: int32 [32, 1], replicated, may hold values from 0 to 3; in each aligned block of 8 rows (0 to 7, 8 to 15, ...) at most 2 rows name the same one
Outputs:
- layer_out: bfloat16 [2048, 1792], P(('group', 'tok'))
- new_states: float32 [32, 273, 1792], P('group', None, 'tok')
- new_norms: float32 [32, 273, 16], P('group')
- new_cache: bfloat16 [32, 2, 1792], P('group', None, 'tok')
The draws below stay inside these ranges and needn't reach their ends.
Inputs may be any that keep to these rules, and one draw needn't show every extreme that they name: `new_lengths`: the 8 lengths of a group sum to 512; in every group at least two requests have one new token and one has exactly 504. `state_source`: among the 8 requests of one group, at most 2 name the same group. For every vector x of 16 entries and every slot and head, phi(x) . cached_norms[slot][:, head] is positive.
All inputs are finite; a program needn't handle non-finite values.
Results may differ from the reference program's by a relative error of at most 0.02.
Values may be sent and summed in bfloat16 or wider, within the bound.
A program may use at most 128 MiB of HBM per device.

```python
import math
import jax
import jax.numpy as jnp
import numpy as np
from jax import lax

D = 1792
H = 16
FD = 16
FF = 4864
KER = 3
CAP = 2
SPAN = 1024
CONTEXT = 32768
REQ_G = 8
PHI = 273
TOKENS_G = 512
TOKENS = 2048
REQS = 32
MOST_NEW = 504
N_GROUP = 4
N_TOK = 8


quad_scale = 0.25 / math.sqrt(2.0)


def draw_cached_norms(key, part):
    key_one, key_two = jax.random.split(key)
    drawn = jax.random.normal(key_one, (REQS, 4, H, FD), jnp.float32)
    low_end = math.log(4.0)
    high_end = math.log(64.0)
    scales = jnp.exp(jax.random.uniform(key_two, (REQS, 4, 1, H), jnp.float32, low_end, high_end))
    ones_part = jnp.ones((REQS, 4, 1, H), jnp.float32)
    linear_part = 0.5 * jnp.transpose(drawn, (0, 1, 3, 2))
    outer_terms = drawn[:, :, :, :, None] * drawn[:, :, :, None, :]
    quad_part = quad_scale * jnp.transpose(outer_terms.reshape(REQS, 4, H, FD * FD), (0, 1, 3, 2))
    features = jnp.concatenate([ones_part, linear_part, quad_part], axis=2)
    return jnp.sum(scales * features, axis=1)


def draw_cached_lengths(key, part):
    key_one, key_two, key_three = jax.random.split(key, 3)
    category = jax.random.randint(key_one, (REQS,), 0, 6)
    long_lengths = jax.random.randint(key_two, (REQS,), 3, CONTEXT - SPAN + 1)
    lengths = jnp.where(category < 3, category, long_lengths)
    places = jax.random.permutation(key_three, REQS)
    lengths = lengths.at[places[0]].set(0)
    lengths = lengths.at[places[1]].set(CONTEXT - SPAN)
    return lengths.astype(jnp.int32)


def group_lengths(key):
    key_one, key_two, key_three = jax.random.split(key, 3)
    shuffled = jax.random.permutation(key_one, REQ_G).astype(jnp.int32)
    ranking = jnp.zeros((REQ_G,), jnp.int32).at[shuffled].set(jnp.arange(REQ_G, dtype=jnp.int32))
    decode_count = jax.random.randint(key_two, (), 2, 4).astype(jnp.int32)
    is_decode = ranking < decode_count
    is_longest = ranking == decode_count
    middle_rows = jnp.logical_not(is_decode | is_longest)
    middle_count = REQ_G - decode_count - 1
    spare_rows = TOKENS_G - decode_count - MOST_NEW - middle_count
    draw_weights = jnp.where(middle_rows, jax.random.randint(key_three, (REQ_G,), 1, 65), 0).astype(jnp.int32)
    extra_rows = (spare_rows * draw_weights // jnp.sum(draw_weights)).astype(jnp.int32)
    room_left = jnp.where(middle_rows, MOST_NEW - 1, 0).astype(jnp.int32)
    extra_rows = jnp.minimum(extra_rows, room_left)
    leftover = spare_rows - jnp.sum(extra_rows)
    free_room = room_left - extra_rows
    before = (jnp.cumsum(free_room) - free_room).astype(jnp.int32)
    extra_rows = extra_rows + jnp.clip(leftover - before, 0, free_room)
    lengths = jnp.where(is_decode, 1, jnp.where(is_longest, MOST_NEW, 1 + extra_rows))
    return lengths.astype(jnp.int32)


def draw_new_lengths(key, part):
    group_keys = jax.random.split(jax.random.fold_in(key, 17), N_GROUP)
    return jax.vmap(group_lengths)(group_keys).astype(jnp.int32)


def levels(rng, shape, pieces, low, largest):
    gain, own = 1.0, jax.random.fold_in(rng, 6)
    for dim, parts in pieces:
        draws = jnp.exp(jax.random.uniform(jax.random.fold_in(own, dim), (parts,), jnp.float32, low / len(pieces), largest / len(pieces)))
        gain = gain * jnp.repeat(draws, shape[dim] // parts).reshape([-1 if axis == dim else 1 for axis in range(len(shape))])
    return gain


def deal_out(own_key, own, number, rows, number_of, top, most, skew):
    order = jax.random.permutation(own_key, number_of)
    packed, common = load_shares(number_of, rows * top, most, skew, True), load_shares(number_of, rows * top, most, skew, False)
    places = jnp.arange(number_of)

    def named(tallies, rotation):
        used = int((tallies > 0).sum())
        fixed = max(1, used // 4)
        shifted = fixed + (places - fixed + rotation * (used - fixed)) % max(1, number_of - fixed)
        return jnp.zeros((number_of,), jnp.int32).at[order[jnp.where(places < fixed, places, shifted)]].set(jnp.asarray(tallies, jnp.int32))

    tallies = jnp.where(number % 4 == 0, named(packed, number // 4), named(common, number - number // 4 - 1))
    mixed = jax.random.permutation(jax.random.fold_in(own, 3), number_of)
    donor, sink = mixed[0:number_of // 2 * 2:2], mixed[1:number_of // 2 * 2:2]
    room = jnp.minimum(tallies[donor] - 1, most - tallies[sink]) // 2
    room = jnp.where((donor == order[0]) | (sink == order[0]) | (tallies[sink] == 0), 0, jnp.maximum(room, 0))
    shifted = jax.random.randint(jax.random.fold_in(own, 4), (number_of // 2,), 0, 1 << 20) % (room + 1)
    tallies = tallies.at[donor].add(-shifted).at[sink].add(shifted)
    items = jnp.searchsorted(jnp.cumsum(tallies), jnp.arange(rows * top), side="right").astype(jnp.int32)
    listing = items.reshape(top, rows).T
    listing = listing[jax.random.permutation(jax.random.fold_in(own, 1), rows)]
    rotation = jax.random.randint(jax.random.fold_in(own, 2), (rows, 1), 0, top)
    return jnp.take_along_axis(listing, (jnp.arange(top)[None, :] + rotation) % top, axis=1)


def load_shares(number_of, total, limit, skew, full):
    weights = [(1 << 20) // math.isqrt(standing ** skew) + 1 for standing in range(1, number_of + 1)]
    largest = limit if full else min(limit, max(-(-total // number_of), total * weights[0] // sum(weights)))
    least = 1 if total - largest >= number_of - 1 else 0
    holding, rest = [largest] + [least] * (number_of - 1), total - largest - least * (number_of - 1)
    while rest > 0:
        movable = [i for i in range(1, number_of) if holding[i] < largest] or [i for i in range(1, number_of) if holding[i] < limit]
        pool, budget = sum([weights[i] for i in movable]), rest
        for i in movable:
            extra = min(limit - holding[i], max(1, budget * weights[i] // pool), rest)
            holding[i] = holding[i] + extra
            rest = rest - extra
    return np.array(holding)


def gaussian(rng, extent, width, limit, shards=(), kind=jnp.bfloat16):
    entries = width * jax.random.normal(rng, extent, jnp.float32)
    if shards:
        entries = entries * levels(rng, extent, shards, -0.22, 0.18)
    return jnp.clip(entries, -limit, limit).astype(kind)


def setup_inputs(seed: int = 0) -> dict:
    streams_of = jax.random.split(jax.random.key(seed), 15)
    tokens = gaussian(streams_of[0], (TOKENS, D), 1.0, 6.0, ((0, 32),))
    norm_gains = jnp.clip(1.0 + 0.15 * jax.random.normal(streams_of[1], (2, D), jnp.float32), 0.25, 1.75)
    qk_weight = gaussian(streams_of[2], (2, H * FD, D), D ** -0.5, 0.125)
    mixer_weight = gaussian(streams_of[3], (3, D, D), D ** -0.5, 0.125, ((1, 8),))
    conv_weight = jnp.clip(jax.random.uniform(streams_of[4], (KER, D), jnp.float32, -1.0, 1.0) * levels(streams_of[4], (KER, D), ((1, 8),), -0.4, 0.0), -1.0, 1.0)
    out_weight = gaussian(streams_of[5], (2, D, D), (2 * D) ** -0.5, 0.09375, ((1, 8),))
    ffn_weight = gaussian(streams_of[6], (2, FF, D), D ** -0.5, 0.125, ((1, 8),))
    down_weight = gaussian(streams_of[7], (FF, D), FF ** -0.5, 0.078125, ((0, 8),))
    cached_states = gaussian(streams_of[8], (REQS, PHI, D), 2.0, 8.0, ((0, 4), (2, 8)), jnp.float32)
    cached_norms = draw_cached_norms(jax.random.fold_in(streams_of[14], 71), 0)
    conv_cache = gaussian(streams_of[10], (REQS, 2, D), 1.0, 6.0, ((0, 4), (2, 8)))
    cached_lengths = draw_cached_lengths(jax.random.fold_in(streams_of[14], 71), 0)
    new_lengths = draw_new_lengths(jax.random.fold_in(streams_of[14], 71), 0)
    state_source_keys = jax.random.split(jax.random.fold_in(streams_of[13], 1), REQS // REQ_G)
    state_source_turns = jax.random.permutation(jax.random.fold_in(streams_of[13], 3), REQS // REQ_G)
    state_source = jax.vmap(lambda own, number: deal_out(jax.random.fold_in(streams_of[13], 2), own, number, REQ_G, N_GROUP, 1, CAP, 2))(state_source_keys, state_source_turns).reshape((REQS, 1))
    return {"tokens": tokens, "norm_gains": norm_gains, "qk_weight": qk_weight, "mixer_weight": mixer_weight, "conv_weight": conv_weight, "out_weight": out_weight, "ffn_weight": ffn_weight, "down_weight": down_weight, "cached_states": cached_states, "cached_norms": cached_norms, "conv_cache": conv_cache, "cached_lengths": cached_lengths, "new_lengths": new_lengths, "state_source": state_source}


epsilon = 1e-05
quad_scale = 0.25 / math.sqrt(2.0)
highest = lax.Precision.HIGHEST

def rms_scale(inputs, gain_row):
    widened = inputs.astype(jnp.float32)
    mean_sq = lax.optimization_barrier(jnp.mean(widened * widened, axis=-1, keepdims=True))
    return widened * lax.rsqrt(mean_sq + epsilon) * gain_row

def taylor_features(vectors):
    row_count = vectors.shape[0]
    feat_count = vectors.shape[1]
    outer_terms = (vectors[:, :, None] * vectors[:, None, :]).reshape(row_count, feat_count * feat_count)
    return jnp.concatenate([jnp.ones((row_count, 1), jnp.float32), 0.5 * vectors, quad_scale * outer_terms], axis=1)

def segment_layout(lengths, all_rows):
    request_ends = jnp.cumsum(lengths).astype(jnp.int32)
    request_starts = (request_ends - lengths).astype(jnp.int32)
    position = jnp.arange(all_rows, dtype=jnp.int32)
    segment = lax.optimization_barrier(jnp.sum((position[:, None] >= request_ends[None, :]).astype(jnp.int32), axis=1)).astype(jnp.int32)
    member = segment[:, None] == jnp.arange(lengths.shape[0], dtype=jnp.int32)[None, :]
    offset = (position - lax.optimization_barrier(jnp.sum(jnp.where(member, request_starts[None, :], 0), axis=1))).astype(jnp.int32)
    return (request_ends, segment, member, offset)

def head_attention(queries, keys_head, values_head, state_head, norm_head, segment, member, query_block):
    all_rows = queries.shape[0]
    requests, phi_size, value_width = state_head.shape
    state_flat = jnp.transpose(state_head, (1, 0, 2)).reshape(phi_size, requests * value_width)
    position = jnp.arange(all_rows, dtype=jnp.int32)
    pieces_out = []
    for first_row in range(0, all_rows, query_block):
        query_rows = queries[first_row:first_row + query_block]
        scores = lax.dot_general(query_rows, keys_head, (((1,), (1,)), ((), ())), precision=highest)
        kernel = 1.0 + 0.25 * scores + scores * scores / 32.0
        allowed = (segment[first_row:first_row + query_block, None] == segment[None, :]) & (position[None, :] <= position[first_row:first_row + query_block, None])
        kernel = jnp.where(allowed, kernel, 0.0)
        local_den = lax.optimization_barrier(jnp.sum(kernel, axis=1))
        local_num = jnp.dot(kernel.astype(jnp.bfloat16), values_head, preferred_element_type=jnp.float32)
        features = taylor_features(query_rows)
        carried = jnp.dot(features, state_flat, precision=highest).reshape(query_block, requests, value_width)
        owner = member[first_row:first_row + query_block]
        carried_num = lax.optimization_barrier(jnp.sum(jnp.where(owner[:, :, None], carried, 0.0), axis=1))
        carried_den = lax.optimization_barrier(jnp.sum(jnp.where(owner, jnp.dot(features, norm_head.T, precision=highest), 0.0), axis=1))
        pieces_out.append((local_num + carried_num) / (local_den + carried_den)[:, None])
    return jnp.concatenate(pieces_out, axis=0).astype(jnp.bfloat16)

def state_update(keys_head, values_head, member, state_head, norm_head):
    all_rows = keys_head.shape[0]
    requests, phi_size, value_width = state_head.shape
    features = taylor_features(keys_head)
    weights = member.astype(jnp.float32)
    spread = (weights[:, :, None] * values_head.astype(jnp.float32)[:, None, :]).reshape(all_rows, requests * value_width)
    added_state = lax.dot_general(features, spread, (((0,), (0,)), ((), ())), precision=highest)
    added_state = jnp.transpose(added_state.reshape(phi_size, requests, value_width), (1, 0, 2))
    norm_added = lax.dot_general(weights, features, (((0,), (0,)), ((), ())), precision=highest)
    return (state_head + added_state, norm_head + norm_added)

def short_conv(inputs, conv_gate, conv_taps, conv_state, cached_length, lengths, request_ends, member, offset):
    all_rows = inputs.shape[0]
    channels = inputs.shape[1]
    cached = conv_state.astype(jnp.float32)
    last_cached = cached[:, 1] * (cached_length >= 1).astype(jnp.float32)[:, None]
    second_cached = cached[:, 0] * (cached_length >= 2).astype(jnp.float32)[:, None]
    last_rows = lax.optimization_barrier(jnp.sum(jnp.where(member[:, :, None], last_cached[None], 0.0), axis=1))
    second_rows = lax.optimization_barrier(jnp.sum(jnp.where(member[:, :, None], second_cached[None], 0.0), axis=1))
    shift_one = jnp.concatenate([jnp.zeros((1, channels), jnp.float32), inputs[:-1]], axis=0)
    shift_two = jnp.concatenate([jnp.zeros((2, channels), jnp.float32), inputs[:-2]], axis=0)
    within = offset[:, None]
    prev_one = jnp.where(within >= 1, shift_one, last_rows)
    prev_two = jnp.where(within >= 2, shift_two, jnp.where(within == 1, last_rows, second_rows))
    convolved = conv_taps[0] * inputs + conv_taps[1] * prev_one + conv_taps[2] * prev_two
    conv_out = (convolved * conv_gate).astype(jnp.bfloat16)
    position = jnp.arange(all_rows, dtype=jnp.int32)
    at_end = position[None, :] == (request_ends - 1)[:, None]
    before_end = position[None, :] == (request_ends - 2)[:, None]
    final_rows = lax.optimization_barrier(jnp.sum(jnp.where(at_end[:, :, None], inputs[None], 0.0), axis=1))
    penultimate = lax.optimization_barrier(jnp.sum(jnp.where(before_end[:, :, None], inputs[None], 0.0), axis=1))
    penultimate = jnp.where((lengths >= 2)[:, None], penultimate, last_cached)
    return (conv_out, jnp.stack([penultimate, final_rows], axis=1).astype(jnp.bfloat16))

def shard_sum(left_rows, right_rows, shard_count):
    shard_width = left_rows.shape[1] // shard_count

    def add_shard(shard_index, running):
        begin = (shard_index * shard_width).astype(jnp.int32)
        left_part = lax.dynamic_slice_in_dim(left_rows, begin, shard_width, 1)
        right_part = lax.dynamic_slice_in_dim(right_rows, begin, shard_width, 0)
        partial_value = jnp.dot(left_part, right_part, preferred_element_type=jnp.float32)
        return running + lax.optimization_barrier(partial_value.astype(jnp.bfloat16)).astype(jnp.float32)
    blank = jnp.zeros((left_rows.shape[0], right_rows.shape[1]), jnp.float32)
    return lax.fori_loop(0, shard_count, add_shard, blank)

def reference(tokens, norm_gains, qk_weight, mixer_weight, conv_weight, out_weight, ffn_weight, down_weight, cached_states, cached_norms, conv_cache, cached_lengths, new_lengths, state_source):
    head_width = D // H
    query_block = math.gcd(TOKENS_G, 512)
    request_slot = (jnp.arange(REQS, dtype=jnp.int32) % REQ_G).astype(jnp.int32)
    slots = (state_source[:, 0] * REQ_G + request_slot).astype(jnp.int32)
    has_state = (cached_lengths > 0).astype(jnp.float32)[:, None, None]
    start_states = cached_states[slots] * has_state
    start_norms = cached_norms[slots] * has_state
    start_cache = conv_cache[slots]
    out_rows = jnp.transpose(out_weight.reshape(2, N_TOK, D // N_TOK, D), (1, 0, 2, 3)).reshape(2 * D, D)
    layer_parts = []
    state_parts = []
    norm_parts = []
    cache_parts = []
    for group_id in range(N_GROUP):
        rows_low = group_id * TOKENS_G
        group_rows = tokens[rows_low:rows_low + TOKENS_G]
        req_low = group_id * REQ_G
        lengths = new_lengths[group_id]
        request_ends, segment, member, offset = segment_layout(lengths, TOKENS_G)
        normed = rms_scale(group_rows, norm_gains[0]).astype(jnp.bfloat16)
        values = jnp.dot(normed, mixer_weight[0].T, preferred_element_type=jnp.float32).astype(jnp.bfloat16)
        conv_in = jnp.dot(normed, mixer_weight[1].T, preferred_element_type=jnp.float32)
        conv_gate = jnp.dot(normed, mixer_weight[2].T, preferred_element_type=jnp.float32)
        queries = jnp.dot(normed, qk_weight[0].T, preferred_element_type=jnp.float32)
        keys_all = jnp.dot(normed, qk_weight[1].T, preferred_element_type=jnp.float32)
        head_queries = jnp.transpose(queries.reshape(TOKENS_G, H, FD), (1, 0, 2))
        head_keys = jnp.transpose(keys_all.reshape(TOKENS_G, H, FD), (1, 0, 2))
        head_values = jnp.transpose(values.reshape(TOKENS_G, H, head_width), (1, 0, 2))
        group_states = start_states[req_low:req_low + REQ_G]
        head_states = jnp.transpose(group_states.reshape(REQ_G, PHI, H, head_width), (2, 0, 1, 3))
        head_norms = jnp.transpose(start_norms[req_low:req_low + REQ_G], (2, 0, 1))

        def one_head(operands):
            query_part, key_part, value_part, state_part, norm_part = operands
            attended_head = head_attention(query_part, key_part, value_part, state_part, norm_part, segment, member, query_block)
            state_next, norm_next = state_update(key_part, value_part, member, state_part, norm_part)
            return (attended_head, state_next, norm_next)
        attended, state_next, norm_next = lax.map(one_head, (head_queries, head_keys, head_values, head_states, head_norms))
        attended = jnp.transpose(attended, (1, 0, 2)).reshape(TOKENS_G, D)
        state_parts.append(jnp.transpose(state_next, (1, 2, 0, 3)).reshape(REQ_G, PHI, D))
        norm_parts.append(jnp.transpose(norm_next, (1, 2, 0)))
        conv_out, cache_next = short_conv(conv_in, conv_gate, conv_weight, start_cache[req_low:req_low + REQ_G], cached_lengths[req_low:req_low + REQ_G], lengths, request_ends, member, offset)
        cache_parts.append(cache_next)
        mixer_in = jnp.stack([attended.reshape(TOKENS_G, N_TOK, D // N_TOK), conv_out.reshape(TOKENS_G, N_TOK, D // N_TOK)], axis=2).reshape(TOKENS_G, 2 * D)
        residual = group_rows.astype(jnp.float32) + shard_sum(mixer_in, out_rows, N_TOK)
        normed_ffn = rms_scale(residual, norm_gains[1]).astype(jnp.bfloat16)
        gate_part = jnp.dot(normed_ffn, ffn_weight[0].T, preferred_element_type=jnp.float32)
        up_part = jnp.dot(normed_ffn, ffn_weight[1].T, preferred_element_type=jnp.float32)
        hidden = (jax.nn.silu(gate_part) * up_part).astype(jnp.bfloat16)
        layer_parts.append((residual + shard_sum(hidden, down_weight, N_TOK)).astype(jnp.bfloat16))
    return (jnp.concatenate(layer_parts, axis=0), jnp.concatenate(state_parts, axis=0), jnp.concatenate(norm_parts, axis=0), jnp.concatenate(cache_parts, axis=0))
```

```python
import math

import jax
import jax.numpy as jnp
import numpy as np
from jax import lax
from jax.experimental import pallas as pl
from jax.experimental.pallas import tpu as pltpu
from jax.sharding import PartitionSpec as P

epsilon = 1e-05
quad_scale = 0.25 / math.sqrt(2.0)
highest = lax.Precision.HIGHEST


def rms_scale(inputs, gain_row):
    widened = inputs.astype(jnp.float32)
    mean_sq = jnp.mean(widened * widened, axis=-1, keepdims=True)
    return widened * lax.rsqrt(mean_sq + epsilon) * gain_row


def taylor_features(vectors):
    row_count = vectors.shape[0]
    feat_count = vectors.shape[1]
    outer_terms = (vectors[:, :, None] * vectors[:, None, :]).reshape(
        row_count, feat_count * feat_count
    )
    return jnp.concatenate(
        [jnp.ones((row_count, 1), jnp.float32), 0.5 * vectors, quad_scale * outer_terms], axis=1
    )


def segment_layout(lengths, all_rows):
    request_ends = jnp.cumsum(lengths)
    request_starts = request_ends - lengths
    position = jnp.arange(all_rows, dtype=jnp.int32)
    segment = jnp.sum((position[:, None] >= request_ends[None, :]).astype(jnp.int32), axis=1)
    member = segment[:, None] == jnp.arange(lengths.shape[0], dtype=jnp.int32)[None, :]
    offset = position - jnp.sum(jnp.where(member, request_starts[None, :], 0), axis=1)
    return (request_ends, segment, member, offset)


def head_attention(
    queries, keys_head, values_head, state_head, norm_head, segment, member, query_block
):
    all_rows = queries.shape[0]
    requests, phi_size, value_width = state_head.shape
    state_flat = jnp.transpose(state_head, (1, 0, 2)).reshape(phi_size, requests * value_width)
    position = jnp.arange(all_rows, dtype=jnp.int32)
    pieces_out = []
    for first_row in range(0, all_rows, query_block):
        query_rows = queries[first_row : first_row + query_block]
        scores = lax.dot_general(query_rows, keys_head, (((1,), (1,)), ((), ())), precision=highest)
        kernel = 1.0 + 0.25 * scores + scores * scores / 32.0
        allowed = (segment[first_row : first_row + query_block, None] == segment[None, :]) & (
            position[None, :] <= position[first_row : first_row + query_block, None]
        )
        kernel = jnp.where(allowed, kernel, 0.0)
        local_den = jnp.sum(kernel, axis=1)
        local_num = jnp.dot(
            kernel.astype(jnp.bfloat16), values_head, preferred_element_type=jnp.float32
        )
        features = taylor_features(query_rows)
        carried = jnp.dot(features, state_flat, precision=highest).reshape(
            query_block, requests, value_width
        )
        owner = member[first_row : first_row + query_block]
        carried_num = jnp.sum(jnp.where(owner[:, :, None], carried, 0.0), axis=1)
        carried_den = jnp.sum(
            jnp.where(owner, jnp.dot(features, norm_head.T, precision=highest), 0.0), axis=1
        )
        pieces_out.append((local_num + carried_num) / (local_den + carried_den)[:, None])
    return jnp.concatenate(pieces_out, axis=0).astype(jnp.bfloat16)


def state_update(keys_head, values_head, member, state_head, norm_head):
    all_rows = keys_head.shape[0]
    requests, phi_size, value_width = state_head.shape
    features = taylor_features(keys_head)
    weights = member.astype(jnp.float32)
    spread = (weights[:, :, None] * values_head.astype(jnp.float32)[:, None, :]).reshape(
        all_rows, requests * value_width
    )
    added_state = lax.dot_general(features, spread, (((0,), (0,)), ((), ())), precision=highest)
    added_state = jnp.transpose(added_state.reshape(phi_size, requests, value_width), (1, 0, 2))
    norm_added = lax.dot_general(weights, features, (((0,), (0,)), ((), ())), precision=highest)
    return (state_head + added_state, norm_head + norm_added)


def short_conv(
    inputs, conv_gate, conv_taps, conv_state, cached_length, lengths, request_ends, member, offset
):
    all_rows = inputs.shape[0]
    channels = inputs.shape[1]
    cached = conv_state.astype(jnp.float32)
    last_cached = cached[:, 1] * (cached_length >= 1).astype(jnp.float32)[:, None]
    second_cached = cached[:, 0] * (cached_length >= 2).astype(jnp.float32)[:, None]
    last_rows = jnp.sum(jnp.where(member[:, :, None], last_cached[None], 0.0), axis=1)
    second_rows = jnp.sum(jnp.where(member[:, :, None], second_cached[None], 0.0), axis=1)
    shift_one = jnp.concatenate([jnp.zeros((1, channels), jnp.float32), inputs[:-1]], axis=0)
    shift_two = jnp.concatenate([jnp.zeros((2, channels), jnp.float32), inputs[:-2]], axis=0)
    within = offset[:, None]
    prev_one = jnp.where(within >= 1, shift_one, last_rows)
    prev_two = jnp.where(within >= 2, shift_two, jnp.where(within == 1, last_rows, second_rows))
    convolved = conv_taps[0] * inputs + conv_taps[1] * prev_one + conv_taps[2] * prev_two
    conv_out = (convolved * conv_gate).astype(jnp.bfloat16)
    position = jnp.arange(all_rows, dtype=jnp.int32)
    at_end = position[None, :] == (request_ends - 1)[:, None]
    before_end = position[None, :] == (request_ends - 2)[:, None]
    final_rows = jnp.sum(jnp.where(at_end[:, :, None], inputs[None], 0.0), axis=1)
    penultimate = jnp.sum(jnp.where(before_end[:, :, None], inputs[None], 0.0), axis=1)
    penultimate = jnp.where((lengths >= 2)[:, None], penultimate, last_cached)
    return (conv_out, jnp.stack([penultimate, final_rows], axis=1).astype(jnp.bfloat16))


def down_term(hidden, down_weight):
    return jnp.dot(hidden, down_weight, preferred_element_type=jnp.float32)


def on_device(
    tokens,
    norm_gains,
    qk_weight,
    mixer_weight,
    conv_weight,
    out_weight,
    ffn_weight,
    down_weight,
    cached_states,
    cached_norms,
    conv_cache,
    cached_lengths,
    new_lengths,
    state_source,
):
    tok_rows = tokens.shape[0]
    model_width = tokens.shape[1]
    shards = lax.axis_size("tok")
    requests = cached_states.shape[0]
    phi_size = cached_states.shape[1]
    columns = cached_states.shape[2]
    head_count = cached_norms.shape[2]
    head_width = model_width // head_count
    feature = qk_weight.shape[1] // head_count
    heads_here = max(1, columns // head_width)
    head_cols = columns // heads_here
    all_rows = tok_rows * shards
    query_block = math.gcd(all_rows, 512)
    group_now = lax.axis_index("group")
    tok_now = lax.axis_index("tok")
    first_head = tok_now * columns // head_width
    sources = state_source[:, 0]
    own_sources = lax.dynamic_slice_in_dim(sources, group_now * requests, requests)
    conv_wide = conv_cache.astype(jnp.float32)
    wanted = own_sources * requests + jnp.arange(requests, dtype=jnp.int32)
    blanks = (
        jnp.zeros_like(cached_states),
        jnp.zeros_like(cached_norms),
        jnp.zeros_like(conv_wide),
    )
    pieces = (
        lax.all_gather(cached_states.astype(jnp.bfloat16), "group", axis=0, tiled=True).astype(
            jnp.float32
        ),
        lax.all_gather(cached_norms.astype(jnp.bfloat16), "group", axis=0, tiled=True).astype(
            jnp.float32
        ),
        lax.all_gather(conv_wide.astype(jnp.bfloat16), "group", axis=0, tiled=True).astype(
            jnp.float32
        ),
    )
    row_count = pieces[0].shape[0]
    inside = (wanted >= 0) & (wanted < row_count)
    row_index = jnp.clip(wanted, 0, row_count - 1)
    fetched_states, fetched_norms, fetched_conv = tuple(
        (
            jnp.where(
                inside.reshape((requests,) + (1,) * (portion.ndim - 1)), portion[row_index], current
            )
            for portion, current in zip(pieces, blanks)
        )
    )
    has_state = (cached_lengths > 0).astype(jnp.float32)[:, None, None]
    start_states = fetched_states * has_state
    start_norms = fetched_norms * has_state
    qk_rows = lax.dynamic_slice_in_dim(
        qk_weight, first_head * feature, heads_here * feature, 1
    ).reshape(2 * heads_here * feature, model_width)
    in_rows = jnp.concatenate([mixer_weight.reshape(3 * columns, model_width), qk_rows], axis=0)
    whole_rows = lax.all_gather(tokens, "tok", axis=0, tiled=True)
    projected = lax.dot_general(
        rms_scale(whole_rows, norm_gains[0]).astype(jnp.bfloat16),
        in_rows,
        (((1,), (1,)), ((), ())),
        preferred_element_type=jnp.float32,
    )
    values = projected[:, :columns].astype(jnp.bfloat16)
    conv_in = projected[:, columns : 2 * columns]
    conv_gate = projected[:, 2 * columns : 3 * columns]
    lengths = new_lengths[0]
    request_ends, segment, member, offset = segment_layout(lengths, all_rows)
    pieces_out = []
    states_out = []
    norm_share = jnp.zeros((requests, phi_size, head_count), jnp.float32)
    for head_slot in range(heads_here):
        query_low = 3 * columns + head_slot * feature
        key_low = 3 * columns + (heads_here + head_slot) * feature
        queries = projected[:, query_low : query_low + feature]
        keys_head = projected[:, key_low : key_low + feature]
        values_head = values[:, head_slot * head_cols : (head_slot + 1) * head_cols]
        state_head = start_states[:, :, head_slot * head_cols : (head_slot + 1) * head_cols]
        norm_head = lax.dynamic_index_in_dim(start_norms, first_head + head_slot, 2, keepdims=False)
        pieces_out.append(
            head_attention(
                queries, keys_head, values_head, state_head, norm_head, segment, member, query_block
            )
        )
        state_next, norm_next = state_update(keys_head, values_head, member, state_head, norm_head)
        states_out.append(state_next)
        head_pick = (jnp.arange(head_count, dtype=jnp.int32) == first_head + head_slot).astype(
            jnp.float32
        )
        norm_share = norm_share + norm_next[:, :, None] * head_pick[None, None, :] * (
            head_cols / head_width
        )
    new_norms = lax.psum(norm_share.astype(jnp.bfloat16), "tok").astype(jnp.float32)
    conv_out, new_cache = short_conv(
        conv_in,
        conv_gate,
        conv_weight,
        fetched_conv,
        cached_lengths,
        lengths,
        request_ends,
        member,
        offset,
    )
    mixer_in = jnp.concatenate([jnp.concatenate(pieces_out, axis=1), conv_out], axis=1)
    out_rows = out_weight.reshape(2 * columns, model_width)
    ffn_units = ffn_weight.shape[1]
    ffn_rows_all = ffn_weight.reshape(2 * ffn_units, model_width)
    mixed_sum = lax.psum(
        jnp.dot(mixer_in, out_rows, preferred_element_type=jnp.float32).astype(jnp.bfloat16), "tok"
    ).astype(jnp.float32)
    residual = whole_rows.astype(jnp.float32) + mixed_sum
    both_parts = lax.dot_general(
        rms_scale(residual, norm_gains[1]).astype(jnp.bfloat16),
        ffn_rows_all,
        (((1,), (1,)), ((), ())),
        preferred_element_type=jnp.float32,
    )
    hidden = (jax.nn.silu(both_parts[:, :ffn_units]) * both_parts[:, ffn_units:]).astype(
        jnp.bfloat16
    )
    residual_own = lax.dynamic_slice_in_dim(residual, tok_now * tok_rows, tok_rows, 0)
    layer_out = (
        residual_own
        + lax.psum_scatter(
            down_term(hidden, down_weight).astype(jnp.bfloat16),
            "tok",
            scatter_dimension=0,
            tiled=True,
        ).astype(jnp.float32)
    ).astype(jnp.bfloat16)
    return (layer_out, jnp.concatenate(states_out, axis=2), new_norms, new_cache)


VMEM = pltpu.VMEM
wide = 256
feat_rows = 288
slot_rows = 304
big_vmem = 56 * 1024 * 1024
f32 = jnp.float32
bf16 = jnp.bfloat16


def dot_nt(left, right):
    return lax.dot_general(left, right, (((1,), (1,)), ((), ())), preferred_element_type=f32)


def dot_nn(left, right):
    return jnp.dot(left, right, preferred_element_type=f32)


def feature_tables(heads, feature):
    parts = 2 * heads
    first = np.zeros((parts, feature * parts, feat_rows), np.float32)
    second = np.zeros((parts, feature * parts, feat_rows), np.float32)
    add = np.zeros((3, feat_rows), np.float32)
    add[0, 0] = 1.0
    add[1, : 1 + feature] = 1.0
    add[2, 0] = 1.0
    add[2, 1 : 1 + feature] = 0.5
    add[2, 1 + feature : 1 + feature + feature * feature] = quad_scale
    for part in range(parts):
        for a in range(feature):
            first[part, part * feature + a, 1 + a] = 1.0
            for b in range(feature):
                entry = 1 + feature + a * feature + b
                first[part, part * feature + a, entry] = 1.0
                second[part, part * feature + b, entry] = 1.0
    return first, second, add


def places():
    me = lax.axis_index("tok")
    core = me % 2
    x = (me // 2) % 2
    y = me // 4
    sib = me + 1 - 2 * core
    xn = me + 2 - 4 * x
    yn = me + 4 - 8 * y
    dg = xn + 4 - 8 * y
    return me, core, sib, (me, xn, yn, dg)


def enter():
    me = lax.axis_index("tok")
    barrier = pltpu.get_barrier_semaphore()
    for step in range(1, 8):
        pl.semaphore_signal(
            barrier,
            inc=1,
            device_id={"tok": (me + step) % 8},
            device_id_type=pl.DeviceIdType.MESH,
        )
    pl.semaphore_wait(barrier, 7)


def remote(src, dst, send, recv, target):
    return pltpu.make_async_remote_copy(
        src_ref=src,
        dst_ref=dst,
        send_sem=send,
        recv_sem=recv,
        device_id={"tok": target},
        device_id_type=pl.DeviceIdType.MESH,
    )


def block_at(ref, index, rows):
    return ref.at[pl.ds(pl.multiple_of(index * rows, rows), rows)]


def gather_rows(own_ref, all_ref, rows, send, recv):
    me, core, sib, peers = places()
    home = block_at(all_ref, me, rows)
    out = []
    for k in (3, 1, 2):
        copy = remote(own_ref, home, send.at[k], recv.at[k], peers[k])
        copy.start()
        out.append(copy)
    copy = remote(own_ref, home, send.at[4], recv.at[4], sib)
    copy.start()
    out.append(copy)
    for k in (1, 2, 3):
        landed = block_at(all_ref, peers[k], rows)
        remote(own_ref, landed, send.at[k], recv.at[k], peers[k]).wait_recv()
        copy = remote(landed, landed, send.at[4 + k], recv.at[4 + k], sib)
        copy.start()
        out.append(copy)
    for k in range(4):
        other = peers[k] + 1 - 2 * core
        landed = block_at(all_ref, other, rows)
        remote(landed, landed, send.at[4 + k], recv.at[4 + k], sib).wait_recv()
    for copy in out:
        copy.wait_send()


def scatter_sum(part_ref, sib_ref, pair_ref, far_ref, rows, send, recv):
    me, core, sib, peers = places()
    out = []
    for k in (3, 1, 2, 0):
        theirs = peers[k] + 1 - 2 * core
        copy = remote(block_at(part_ref, theirs, rows), sib_ref.at[k], send.at[k], recv.at[k], sib)
        copy.start()
        out.append(copy)
    for place, k in enumerate((3, 1, 2)):
        out[place].wait_recv()
        pair_ref[k] = (
            block_at(part_ref, peers[k], rows)[...].astype(f32) + sib_ref[k].astype(f32)
        ).astype(bf16)
        copy = remote(pair_ref.at[k], far_ref.at[k], send.at[4 + k], recv.at[4 + k], peers[k])
        copy.start()
        out.append(copy)
    out[3].wait_recv()
    total = block_at(part_ref, me, rows)[...].astype(f32) + sib_ref[0].astype(f32)
    for place, k in enumerate((3, 1, 2)):
        out[4 + place].wait_recv()
    for k in (1, 2, 3):
        total = total + far_ref[k].astype(f32)
    for copy in out:
        copy.wait_send()
    return total


def token_kernel(own_ref, all_ref, held, send, recv, local):
    rows = own_ref.shape[0]
    enter()
    me = lax.axis_index("tok")
    copy = pltpu.make_async_copy(own_ref, block_at(held, me, rows), local)
    copy.start()
    gather_rows(own_ref, held, rows, send, recv)
    copy.wait()
    all_ref[...] = held[...]


def pick_kernel(slot_ref, state_ref, norm_ref, conv_ref, out_ref):
    phi_size, columns = state_ref.shape[1], state_ref.shape[2]
    head_count = norm_ref.shape[2]
    heads = slot_ref[8]
    row = lax.broadcasted_iota(jnp.int32, (head_count, wide), 0)
    col = lax.broadcasted_iota(jnp.int32, (head_count, wide), 1)
    choose = ((col >= columns) & (col < columns + 2) & (row == heads + col - columns)).astype(f32)
    out_ref[0] = jnp.zeros((slot_rows, wide), bf16)
    out_ref[0, 0:phi_size, :] = dot_nn(
        norm_ref[0].astype(bf16), choose.astype(bf16)
    ).astype(bf16)
    out_ref[0, 0:phi_size, 0:columns] = state_ref[0].astype(bf16)
    out_ref[0, feat_rows : feat_rows + 2, 0:columns] = conv_ref[0]


def head_zero(shape, columns):
    col = lax.broadcasted_iota(jnp.int32, shape, 1)
    return (col < columns // 2) | (col == columns)


def local_kernel(
    info_ref, rows_ref, gain_ref, mixer_ref, qk_ref, qk_out, v_out, conv_out, gate_out, acc_out, normed
):
    all_rows = rows_ref.shape[0]
    columns = mixer_ref.shape[1]
    feature = 16
    half = 256

    @pl.loop(0, all_rows // half)
    def _(step):
        span = pl.ds(pl.multiple_of(step * half, half), half)
        x = rows_ref[span, :].astype(f32)
        scale = lax.rsqrt(jnp.mean(x * x, axis=-1, keepdims=True) + epsilon)
        normed[...] = (x * scale * gain_ref[0:1, :]).astype(bf16)
        v_out[span, :] = jnp.ones((half, wide), bf16)
        v_out[span, 0:columns] = dot_nt(normed[...], mixer_ref[0]).astype(bf16)
        conv_out[span, :] = dot_nt(normed[...], mixer_ref[1])
        gate_out[span, :] = dot_nt(normed[...], mixer_ref[2])
        qk_out[span, :] = dot_nt(normed[...], qk_ref[...].reshape(4 * feature, qk_ref.shape[2]))

    block = 128

    @pl.loop(0, all_rows // block)
    def _(step):
        low = pl.multiple_of(step * block, block)
        span = pl.ds(low, block)
        query = qk_out[span, :]
        i = lax.broadcasted_iota(jnp.int32, (block, 1), 0) + low
        begin = jnp.zeros((block, 1), jnp.int32)
        for r in range(8):
            begin = jnp.where(i >= info_ref[r], info_ref[r], begin)
        j = lax.broadcasted_iota(jnp.int32, (block, all_rows), 1)
        allowed = (j <= i) & (j >= begin)
        found = []
        for h in range(2):
            q = query[:, h * feature : (h + 1) * feature].astype(bf16)
            k = qk_out[:, (2 + h) * feature : (3 + h) * feature].astype(bf16)
            s = dot_nt(q, k)
            w = jnp.where(allowed, 1.0 + 0.25 * s + s * s * (1.0 / 32.0), 0.0).astype(bf16)
            found.append(dot_nn(w, v_out[...]))
        acc_out[span, :] = jnp.where(head_zero((block, wide), columns), found[0], found[1])


def carried_kernel(
    info_ref,
    qk_ref,
    v_ref,
    conv_ref,
    gate_ref,
    acc_ref,
    slots_a,
    slots_b,
    slots_c,
    slots_d,
    first_ref,
    second_ref,
    add_ref,
    first_t_ref,
    second_t_ref,
    add_t_ref,
    taps_ref,
    weight_ref,
    mixed_out,
    state_out,
    norm_out,
    cache_out,
    num,
    shifted,
    prev_one,
    prev_two,
    phi_q,
    phi_k,
    att,
):
    all_rows, columns = conv_ref.shape
    phi_size = state_out.shape[1]
    hi = qk_ref[...].astype(bf16)
    lo = (qk_ref[...] - hi.astype(f32)).astype(bf16)
    for h in range(2):
        one = dot_nn(hi, first_ref[h]) + dot_nn(lo, first_ref[h]) + add_ref[0:1]
        two = dot_nn(hi, second_ref[h]) + dot_nn(lo, second_ref[h]) + add_ref[1:2]
        phi_q[h] = (one * two * add_ref[2:3]).astype(bf16)
        one = dot_nt(first_t_ref[h], hi) + dot_nt(first_t_ref[h], lo) + add_t_ref[:, 0:1]
        two = dot_nt(second_t_ref[h], hi) + dot_nt(second_t_ref[h], lo) + add_t_ref[:, 1:2]
        phi_k[h] = (one * two * add_t_ref[:, 2:3]).astype(bf16)
    num[...] = acc_ref[...]
    shifted[0:8, :] = jnp.zeros((8, columns), f32)
    shifted[8 : 8 + all_rows, :] = conv_ref[...]
    prev_one[...] = shifted[7 : 7 + all_rows, :]
    prev_two[...] = shifted[6 : 6 + all_rows, :]
    i = lax.broadcasted_iota(jnp.int32, (all_rows, 1), 0)
    row_zero = head_zero((all_rows, wide), columns)
    state_zero = head_zero((feat_rows, wide), columns)
    for index in range(8):
        slots = (slots_a, slots_b, slots_c, slots_d)[index // 2]
        request = info_ref[24 + index]
        begin = info_ref[request]
        length = info_ref[8 + request]
        cached = info_ref[16 + request]
        end = begin + length
        live = jnp.where(cached > 0, 1.0, 0.0).astype(f32)
        state = slots[index % 2, 0:feat_rows, :]
        member = (i >= begin) & (i < end)
        carried = jnp.where(row_zero, dot_nn(phi_q[0], state), dot_nn(phi_q[1], state)) * live
        num[...] += jnp.where(member, carried, 0.0)
        mine = jnp.where(member, v_ref[...].astype(f32), 0.0).astype(bf16)
        added = jnp.where(state_zero, dot_nn(phi_k[0], mine), dot_nn(phi_k[1], mine))
        fresh = state.astype(f32) * live + added
        state_out[request] = fresh[0:phi_size, 0:columns]
        norm_out[request] = fresh[0:feat_rows, 128:256]
        tail = slots[index % 2, feat_rows:slot_rows, 0:columns].astype(f32)
        newest = tail[1:2] * live
        oldest = tail[0:1] * jnp.where(cached >= 2, 1.0, 0.0).astype(f32)
        prev_one[...] = jnp.where(i == begin, newest, prev_one[...])
        prev_two[...] = jnp.where(
            i == begin, oldest, jnp.where((i == begin + 1) & (i < end), newest, prev_two[...])
        )
        final = shifted[pl.ds(7 + end, 1), :]
        before = shifted[pl.ds(6 + end, 1), :]
        cache_out[request, 0:1, :] = jnp.where(length >= 2, before, newest)
        cache_out[request, 1:2, :] = final
    col = lax.broadcasted_iota(jnp.int32, (all_rows, wide), 1)
    den = jnp.where(col < columns // 2, num[:, columns : columns + 1], num[:, columns + 1 : columns + 2])
    att[...] = (num[...] / den).astype(bf16)
    convolved = (
        taps_ref[0:1] * conv_ref[...] + taps_ref[1:2] * prev_one[...] + taps_ref[2:3] * prev_two[...]
    )
    gated = (convolved * gate_ref[...]).astype(bf16)
    prev_one[...] = gated.astype(f32)

    @pl.loop(0, all_rows // 256)
    def _(step):
        span = pl.ds(pl.multiple_of(step * 256, 256), 256)
        mixed_out[span, :] = (
            dot_nn(att[span, 0:columns], weight_ref[0])
            + dot_nn(prev_one[span, :].astype(bf16), weight_ref[1])
        ).astype(bf16)


def ffn_kernel(
    part_ref,
    own_ref,
    gain_ref,
    norm_ref,
    up_hbm,
    down_hbm,
    out_ref,
    norms_out,
    up,
    down,
    sib_a,
    pair_a,
    far_a,
    sib_b,
    pair_b,
    far_b,
    own_normed,
    normed,
    part_two,
    norms,
    send_a,
    recv_a,
    send_b,
    recv_b,
    send_g,
    recv_g,
    send_n,
    recv_n,
    load,
):
    rows = own_ref.shape[0]
    all_rows = part_ref.shape[0]
    up_copy = pltpu.make_async_copy(up_hbm, up, load.at[0])
    down_copy = pltpu.make_async_copy(down_hbm, down, load.at[1])
    up_copy.start()
    down_copy.start()
    enter()
    me = lax.axis_index("tok")
    small = []
    total = scatter_sum(part_ref, sib_a, pair_a, far_a, rows, send_a, recv_a)
    residual = own_ref[...].astype(f32) + total
    scale = lax.rsqrt(jnp.mean(residual * residual, axis=-1, keepdims=True) + epsilon)
    own_normed[...] = (residual * scale * gain_ref[1:2, :]).astype(bf16)
    mine = pltpu.make_async_copy(own_normed, block_at(normed, me, rows), load.at[2])
    mine.start()
    gather_rows(own_normed, normed, rows, send_g, recv_g)
    for step in range(1, 8):
        copy = remote(
            norm_ref, norms.at[me], send_n.at[step - 1], recv_n.at[step - 1], (me + step) % 8
        )
        copy.start()
        small.append(copy)
    norms[me] = norm_ref[...]
    mine.wait()
    up_copy.wait()
    down_copy.wait()
    half = 256

    @pl.loop(0, all_rows // half)
    def _(step):
        span = pl.ds(pl.multiple_of(step * half, half), half)
        gate = dot_nt(normed[span, :], up[0])
        lift = dot_nt(normed[span, :], up[1])
        hidden = (gate / (1.0 + jnp.exp(-gate)) * lift).astype(bf16)
        part_two[span, :] = dot_nn(hidden, down[...]).astype(bf16)

    total = scatter_sum(part_two, sib_b, pair_b, far_b, rows, send_b, recv_b)
    out_ref[...] = (residual + total).astype(bf16)
    for step in range(1, 8):
        small[step - 1].wait_send()
        remote(
            norm_ref,
            norms.at[(me + 8 - step) % 8],
            send_n.at[step - 1],
            recv_n.at[step - 1],
            (me + step) % 8,
        ).wait_recv()
    norms_out[...] = norms[...]


def fast_device(
    tokens,
    norm_gains,
    qk_weight,
    mixer_weight,
    conv_weight,
    out_weight,
    ffn_weight,
    down_weight,
    cached_states,
    cached_norms,
    conv_cache,
    cached_lengths,
    new_lengths,
    state_source,
):
    rows, width = tokens.shape
    all_rows = 8 * rows
    requests, phi_size, columns = cached_states.shape
    head_count = cached_norms.shape[2]
    feature = qk_weight.shape[1] // head_count
    heads = 2
    groups = lax.axis_size("group")
    group_now = lax.axis_index("group")
    tok_now = lax.axis_index("tok")
    shape = jax.ShapeDtypeStruct
    dma = pltpu.SemaphoreType.DMA
    in_vmem = pl.BlockSpec(memory_space=VMEM)
    in_smem = pl.BlockSpec(memory_space=pltpu.SMEM)

    sources = state_source[:, 0].reshape(groups, requests)
    request = jnp.arange(requests, dtype=jnp.int32)
    shift = jnp.arange(groups, dtype=jnp.int32)

    def ends_of(match):
        low = jnp.min(jnp.where(match, request[None], requests - 1), axis=1)
        high = jnp.max(jnp.where(match, request[None], 0), axis=1)
        return jnp.stack([low, high], axis=1).reshape(-1).astype(jnp.int32)

    give = ends_of(sources[(group_now + shift) % groups] == group_now)
    own_sources = lax.dynamic_index_in_dim(sources, group_now, 0, keepdims=False)
    take = ends_of(own_sources[None] == ((group_now + groups - shift) % groups)[:, None])
    lengths = new_lengths[0]
    starts = jnp.cumsum(lengths) - lengths
    info = jnp.concatenate([starts, lengths, cached_lengths, take]).astype(jnp.int32)
    picks = jnp.concatenate([give, (tok_now * heads)[None].astype(jnp.int32)])

    packed = pl.pallas_call(
        pick_kernel,
        grid_spec=pltpu.PrefetchScalarGridSpec(
            num_scalar_prefetch=1,
            grid=(2 * groups,),
            in_specs=[
                pl.BlockSpec((1, phi_size, columns), lambda i, s: (s[i], 0, 0)),
                pl.BlockSpec((1, phi_size, head_count), lambda i, s: (s[i], 0, 0)),
                pl.BlockSpec((1, 2, columns), lambda i, s: (s[i], 0, 0)),
            ],
            out_specs=pl.BlockSpec((1, slot_rows, wide), lambda i, s: (i, 0, 0)),
        ),
        out_shape=shape((2 * groups, slot_rows, wide), bf16),
        name="pick_slots",
    )(picks, cached_states, cached_norms, conv_cache)
    arrived = [packed[0:2]]
    for step in range(1, groups):
        ring = [(g, (g + step) % groups) for g in range(groups)]
        arrived.append(lax.ppermute(packed[2 * step : 2 * step + 2], "group", ring))

    whole_rows = pl.pallas_call(
        token_kernel,
        out_shape=shape((all_rows, width), bf16),
        in_specs=[in_vmem],
        out_specs=in_vmem,
        scratch_shapes=[VMEM((all_rows, width), bf16), dma((8,)), dma((8,)), dma],
        compiler_params=pltpu.CompilerParams(
            collective_id=0, has_side_effects=True, vmem_limit_bytes=big_vmem
        ),
        cost_estimate=pl.CostEstimate(flops=0, bytes_accessed=30000000, transcendentals=0),
        name="gather_tokens",
    )(tokens)

    def full(*dims):
        return pl.BlockSpec(dims, lambda i, s: (0,) * len(dims))

    tok_pick = jnp.concatenate([info, tok_now[None].astype(jnp.int32)])
    qk, vext, conv_in, gate, acc = pl.pallas_call(
        local_kernel,
        grid_spec=pltpu.PrefetchScalarGridSpec(
            num_scalar_prefetch=1,
            grid=(1,),
            in_specs=[
                full(all_rows, width),
                full(2, width),
                full(3, columns, width),
                pl.BlockSpec((2, heads * feature, width), lambda i, s: (0, s[32], 0)),
            ],
            out_specs=[
                full(all_rows, 4 * feature),
                full(all_rows, wide),
                full(all_rows, columns),
                full(all_rows, columns),
                full(all_rows, wide),
            ],
            scratch_shapes=[VMEM((256, width), bf16)],
        ),
        out_shape=[
            shape((all_rows, 4 * feature), f32),
            shape((all_rows, wide), bf16),
            shape((all_rows, columns), f32),
            shape((all_rows, columns), f32),
            shape((all_rows, wide), f32),
        ],
        compiler_params=pltpu.CompilerParams(vmem_limit_bytes=big_vmem),
        cost_estimate=pl.CostEstimate(flops=2000000000, bytes_accessed=30000000, transcendentals=0),
        name="local_attention",
    )(tok_pick, whole_rows, norm_gains, mixer_weight, qk_weight)

    first, second, add = feature_tables(heads, feature)
    mixed, new_states, norm_wide, cache_next = pl.pallas_call(
        carried_kernel,
        in_specs=[in_smem] + [in_vmem] * 17,
        out_specs=[in_vmem] * 4,
        out_shape=[
            shape((all_rows, width), bf16),
            shape((requests, phi_size, columns), f32),
            shape((requests, feat_rows, 128), f32),
            shape((requests, 2, columns), f32),
        ],
        scratch_shapes=[
            VMEM((all_rows, wide), f32),
            VMEM((all_rows + 8, columns), f32),
            VMEM((all_rows, columns), f32),
            VMEM((all_rows, columns), f32),
            VMEM((2, all_rows, feat_rows), bf16),
            VMEM((2, feat_rows, all_rows), bf16),
            VMEM((all_rows, wide), bf16),
        ],
        compiler_params=pltpu.CompilerParams(vmem_limit_bytes=big_vmem),
        name="carried_states",
    )(
        info,
        qk,
        vext,
        conv_in,
        gate,
        acc,
        *arrived,
        jnp.asarray(first[:heads], bf16),
        jnp.asarray(second[:heads], bf16),
        jnp.asarray(add, f32),
        jnp.asarray(first[heads:].transpose(0, 2, 1), bf16),
        jnp.asarray(second[heads:].transpose(0, 2, 1), bf16),
        jnp.asarray(add.T, f32),
        conv_weight,
        out_weight,
    )
    low = columns - 128
    share = norm_wide[:, :, low : low + heads].astype(bf16)
    share = jnp.transpose(share, (2, 0, 1)).reshape(heads * requests, feat_rows)
    share = jnp.pad(share, ((0, 0), (0, 384 - feat_rows)))

    units = ffn_weight.shape[1]
    blocks = VMEM((4, rows, width), bf16)
    in_any = pl.BlockSpec(memory_space=pl.ANY)
    layer_out, norms = pl.pallas_call(
        ffn_kernel,
        in_specs=[in_vmem, in_vmem, in_vmem, in_vmem, in_any, in_any],
        out_specs=[in_vmem, in_vmem],
        out_shape=[shape((rows, width), bf16), shape((8,) + share.shape, bf16)],
        scratch_shapes=[
            VMEM((2, units, width), bf16),
            VMEM((units, width), bf16),
            blocks,
            blocks,
            blocks,
            blocks,
            blocks,
            blocks,
            VMEM((rows, width), bf16),
            VMEM((all_rows, width), bf16),
            VMEM((all_rows, width), bf16),
            VMEM((8,) + share.shape, bf16),
        ]
        + [dma((8,))] * 8
        + [dma((3,))],
        compiler_params=pltpu.CompilerParams(
            collective_id=1, has_side_effects=True, vmem_limit_bytes=big_vmem
        ),
        name="sum_and_ffn",
    )(mixed, tokens, norm_gains, share, ffn_weight, down_weight)
    norms = norms.reshape(8, heads, requests, -1)[:, :, :, :phi_size].astype(f32)
    new_norms = jnp.transpose(norms, (2, 3, 0, 1)).reshape(requests, phi_size, head_count)
    return (layer_out, new_states, new_norms, cache_next.astype(bf16))


def device_function(mesh):
    if dict(mesh.shape) == {"group": 4, "tok": 8}:
        return fast_device
    return on_device


def solution(mesh):
    in_specs = (
        P(("group", "tok"), None),
        P(),
        P(),
        P(None, "tok", None),
        P(None, "tok"),
        P(None, "tok", None),
        P(None, "tok", None),
        P("tok", None),
        P("group", None, "tok"),
        P("group", None, None),
        P("group", None, "tok"),
        P("group"),
        P("group", None),
        P(),
    )
    out_specs = (
        P(("group", "tok"), None),
        P("group", None, "tok"),
        P("group", None, None),
        P("group", None, "tok"),
    )
    return jax.shard_map(
        device_function(mesh), mesh=mesh, in_specs=in_specs, out_specs=out_specs, check_vma=False
    )
```

```python
import functools
import math

import jax
import jax.numpy as jnp
import numpy as np
from jax import lax
from jax.experimental import pallas as pl
from jax.experimental.pallas import tpu as pltpu
from jax.sharding import PartitionSpec as P

epsilon = 1e-05
quad_scale = 0.25 / math.sqrt(2.0)
highest = lax.Precision.HIGHEST


def rms_scale(inputs, gain_row):
    widened = inputs.astype(jnp.float32)
    mean_sq = jnp.mean(widened * widened, axis=-1, keepdims=True)
    return widened * lax.rsqrt(mean_sq + epsilon) * gain_row


def taylor_features(vectors):
    row_count = vectors.shape[0]
    feat_count = vectors.shape[1]
    outer_terms = (vectors[:, :, None] * vectors[:, None, :]).reshape(
        row_count, feat_count * feat_count
    )
    return jnp.concatenate(
        [jnp.ones((row_count, 1), jnp.float32), 0.5 * vectors, quad_scale * outer_terms], axis=1
    )


def segment_layout(lengths, all_rows):
    request_ends = jnp.cumsum(lengths)
    request_starts = request_ends - lengths
    position = jnp.arange(all_rows, dtype=jnp.int32)
    segment = jnp.sum((position[:, None] >= request_ends[None, :]).astype(jnp.int32), axis=1)
    member = segment[:, None] == jnp.arange(lengths.shape[0], dtype=jnp.int32)[None, :]
    offset = position - jnp.sum(jnp.where(member, request_starts[None, :], 0), axis=1)
    return (request_ends, segment, member, offset)


def head_attention(
    queries, keys_head, values_head, state_head, norm_head, segment, member, query_block
):
    all_rows = queries.shape[0]
    requests, phi_size, value_width = state_head.shape
    state_flat = jnp.transpose(state_head, (1, 0, 2)).reshape(phi_size, requests * value_width)
    position = jnp.arange(all_rows, dtype=jnp.int32)
    pieces_out = []
    for first_row in range(0, all_rows, query_block):
        query_rows = queries[first_row : first_row + query_block]
        scores = lax.dot_general(query_rows, keys_head, (((1,), (1,)), ((), ())), precision=highest)
        kernel = 1.0 + 0.25 * scores + scores * scores / 32.0
        allowed = (segment[first_row : first_row + query_block, None] == segment[None, :]) & (
            position[None, :] <= position[first_row : first_row + query_block, None]
        )
        kernel = jnp.where(allowed, kernel, 0.0)
        local_den = jnp.sum(kernel, axis=1)
        local_num = jnp.dot(
            kernel.astype(jnp.bfloat16), values_head, preferred_element_type=jnp.float32
        )
        features = taylor_features(query_rows)
        carried = jnp.dot(features, state_flat, precision=highest).reshape(
            query_block, requests, value_width
        )
        owner = member[first_row : first_row + query_block]
        carried_num = jnp.sum(jnp.where(owner[:, :, None], carried, 0.0), axis=1)
        carried_den = jnp.sum(
            jnp.where(owner, jnp.dot(features, norm_head.T, precision=highest), 0.0), axis=1
        )
        pieces_out.append((local_num + carried_num) / (local_den + carried_den)[:, None])
    return jnp.concatenate(pieces_out, axis=0).astype(jnp.bfloat16)


def state_update(keys_head, values_head, member, state_head, norm_head):
    all_rows = keys_head.shape[0]
    requests, phi_size, value_width = state_head.shape
    features = taylor_features(keys_head)
    weights = member.astype(jnp.float32)
    spread = (weights[:, :, None] * values_head.astype(jnp.float32)[:, None, :]).reshape(
        all_rows, requests * value_width
    )
    added_state = lax.dot_general(features, spread, (((0,), (0,)), ((), ())), precision=highest)
    added_state = jnp.transpose(added_state.reshape(phi_size, requests, value_width), (1, 0, 2))
    norm_added = lax.dot_general(weights, features, (((0,), (0,)), ((), ())), precision=highest)
    return (state_head + added_state, norm_head + norm_added)


def short_conv(
    inputs, conv_gate, conv_taps, conv_state, cached_length, lengths, request_ends, member, offset
):
    all_rows = inputs.shape[0]
    channels = inputs.shape[1]
    cached = conv_state.astype(jnp.float32)
    last_cached = cached[:, 1] * (cached_length >= 1).astype(jnp.float32)[:, None]
    second_cached = cached[:, 0] * (cached_length >= 2).astype(jnp.float32)[:, None]
    last_rows = jnp.sum(jnp.where(member[:, :, None], last_cached[None], 0.0), axis=1)
    second_rows = jnp.sum(jnp.where(member[:, :, None], second_cached[None], 0.0), axis=1)
    shift_one = jnp.concatenate([jnp.zeros((1, channels), jnp.float32), inputs[:-1]], axis=0)
    shift_two = jnp.concatenate([jnp.zeros((2, channels), jnp.float32), inputs[:-2]], axis=0)
    within = offset[:, None]
    prev_one = jnp.where(within >= 1, shift_one, last_rows)
    prev_two = jnp.where(within >= 2, shift_two, jnp.where(within == 1, last_rows, second_rows))
    convolved = conv_taps[0] * inputs + conv_taps[1] * prev_one + conv_taps[2] * prev_two
    conv_out = (convolved * conv_gate).astype(jnp.bfloat16)
    position = jnp.arange(all_rows, dtype=jnp.int32)
    at_end = position[None, :] == (request_ends - 1)[:, None]
    before_end = position[None, :] == (request_ends - 2)[:, None]
    final_rows = jnp.sum(jnp.where(at_end[:, :, None], inputs[None], 0.0), axis=1)
    penultimate = jnp.sum(jnp.where(before_end[:, :, None], inputs[None], 0.0), axis=1)
    penultimate = jnp.where((lengths >= 2)[:, None], penultimate, last_cached)
    return (conv_out, jnp.stack([penultimate, final_rows], axis=1).astype(jnp.bfloat16))


def down_term(hidden, down_weight):
    return jnp.dot(hidden, down_weight, preferred_element_type=jnp.float32)


def on_device(
    tokens,
    norm_gains,
    qk_weight,
    mixer_weight,
    conv_weight,
    out_weight,
    ffn_weight,
    down_weight,
    cached_states,
    cached_norms,
    conv_cache,
    cached_lengths,
    new_lengths,
    state_source,
):
    tok_rows = tokens.shape[0]
    model_width = tokens.shape[1]
    shards = lax.axis_size("tok")
    requests = cached_states.shape[0]
    phi_size = cached_states.shape[1]
    columns = cached_states.shape[2]
    head_count = cached_norms.shape[2]
    head_width = model_width // head_count
    feature = qk_weight.shape[1] // head_count
    heads_here = max(1, columns // head_width)
    head_cols = columns // heads_here
    all_rows = tok_rows * shards
    query_block = math.gcd(all_rows, 512)
    group_now = lax.axis_index("group")
    tok_now = lax.axis_index("tok")
    first_head = tok_now * columns // head_width
    sources = state_source[:, 0]
    own_sources = lax.dynamic_slice_in_dim(sources, group_now * requests, requests)
    conv_wide = conv_cache.astype(jnp.float32)
    wanted = own_sources * requests + jnp.arange(requests, dtype=jnp.int32)
    blanks = (
        jnp.zeros_like(cached_states),
        jnp.zeros_like(cached_norms),
        jnp.zeros_like(conv_wide),
    )
    pieces = (
        lax.all_gather(cached_states.astype(jnp.bfloat16), "group", axis=0, tiled=True).astype(
            jnp.float32
        ),
        lax.all_gather(cached_norms.astype(jnp.bfloat16), "group", axis=0, tiled=True).astype(
            jnp.float32
        ),
        lax.all_gather(conv_wide.astype(jnp.bfloat16), "group", axis=0, tiled=True).astype(
            jnp.float32
        ),
    )
    row_count = pieces[0].shape[0]
    inside = (wanted >= 0) & (wanted < row_count)
    row_index = jnp.clip(wanted, 0, row_count - 1)
    fetched_states, fetched_norms, fetched_conv = tuple(
        (
            jnp.where(
                inside.reshape((requests,) + (1,) * (portion.ndim - 1)), portion[row_index], current
            )
            for portion, current in zip(pieces, blanks)
        )
    )
    has_state = (cached_lengths > 0).astype(jnp.float32)[:, None, None]
    start_states = fetched_states * has_state
    start_norms = fetched_norms * has_state
    qk_rows = lax.dynamic_slice_in_dim(
        qk_weight, first_head * feature, heads_here * feature, 1
    ).reshape(2 * heads_here * feature, model_width)
    in_rows = jnp.concatenate([mixer_weight.reshape(3 * columns, model_width), qk_rows], axis=0)
    whole_rows = lax.all_gather(tokens, "tok", axis=0, tiled=True)
    projected = lax.dot_general(
        rms_scale(whole_rows, norm_gains[0]).astype(jnp.bfloat16),
        in_rows,
        (((1,), (1,)), ((), ())),
        preferred_element_type=jnp.float32,
    )
    values = projected[:, :columns].astype(jnp.bfloat16)
    conv_in = projected[:, columns : 2 * columns]
    conv_gate = projected[:, 2 * columns : 3 * columns]
    lengths = new_lengths[0]
    request_ends, segment, member, offset = segment_layout(lengths, all_rows)
    pieces_out = []
    states_out = []
    norm_share = jnp.zeros((requests, phi_size, head_count), jnp.float32)
    for head_slot in range(heads_here):
        query_low = 3 * columns + head_slot * feature
        key_low = 3 * columns + (heads_here + head_slot) * feature
        queries = projected[:, query_low : query_low + feature]
        keys_head = projected[:, key_low : key_low + feature]
        values_head = values[:, head_slot * head_cols : (head_slot + 1) * head_cols]
        state_head = start_states[:, :, head_slot * head_cols : (head_slot + 1) * head_cols]
        norm_head = lax.dynamic_index_in_dim(start_norms, first_head + head_slot, 2, keepdims=False)
        pieces_out.append(
            head_attention(
                queries, keys_head, values_head, state_head, norm_head, segment, member, query_block
            )
        )
        state_next, norm_next = state_update(keys_head, values_head, member, state_head, norm_head)
        states_out.append(state_next)
        head_pick = (jnp.arange(head_count, dtype=jnp.int32) == first_head + head_slot).astype(
            jnp.float32
        )
        norm_share = norm_share + norm_next[:, :, None] * head_pick[None, None, :] * (
            head_cols / head_width
        )
    new_norms = lax.psum(norm_share.astype(jnp.bfloat16), "tok").astype(jnp.float32)
    conv_out, new_cache = short_conv(
        conv_in,
        conv_gate,
        conv_weight,
        fetched_conv,
        cached_lengths,
        lengths,
        request_ends,
        member,
        offset,
    )
    mixer_in = jnp.concatenate([jnp.concatenate(pieces_out, axis=1), conv_out], axis=1)
    out_rows = out_weight.reshape(2 * columns, model_width)
    ffn_units = ffn_weight.shape[1]
    ffn_rows_all = ffn_weight.reshape(2 * ffn_units, model_width)
    mixed_sum = lax.psum(
        jnp.dot(mixer_in, out_rows, preferred_element_type=jnp.float32).astype(jnp.bfloat16), "tok"
    ).astype(jnp.float32)
    residual = whole_rows.astype(jnp.float32) + mixed_sum
    both_parts = lax.dot_general(
        rms_scale(residual, norm_gains[1]).astype(jnp.bfloat16),
        ffn_rows_all,
        (((1,), (1,)), ((), ())),
        preferred_element_type=jnp.float32,
    )
    hidden = (jax.nn.silu(both_parts[:, :ffn_units]) * both_parts[:, ffn_units:]).astype(
        jnp.bfloat16
    )
    residual_own = lax.dynamic_slice_in_dim(residual, tok_now * tok_rows, tok_rows, 0)
    layer_out = (
        residual_own
        + lax.psum_scatter(
            down_term(hidden, down_weight).astype(jnp.bfloat16),
            "tok",
            scatter_dimension=0,
            tiled=True,
        ).astype(jnp.float32)
    ).astype(jnp.bfloat16)
    return (layer_out, jnp.concatenate(states_out, axis=2), new_norms, new_cache)


VMEM = pltpu.VMEM
wide = 256
feat_rows = 288
slot_rows = 304
big_vmem = 56 * 1024 * 1024
f32 = jnp.float32
bf16 = jnp.bfloat16


def dot_nt(left, right):
    return lax.dot_general(left, right, (((1,), (1,)), ((), ())), preferred_element_type=f32)


def dot_nn(left, right):
    return jnp.dot(left, right, preferred_element_type=f32)


def feature_tables(heads, feature):
    parts = 2 * heads
    first = np.zeros((parts, feature * parts, feat_rows), np.float32)
    second = np.zeros((parts, feature * parts, feat_rows), np.float32)
    add = np.zeros((3, feat_rows), np.float32)
    add[0, 0] = 1.0
    add[1, : 1 + feature] = 1.0
    add[2, 0] = 1.0
    add[2, 1 : 1 + feature] = 0.5
    add[2, 1 + feature : 1 + feature + feature * feature] = quad_scale
    for part in range(parts):
        for a in range(feature):
            first[part, part * feature + a, 1 + a] = 1.0
            for b in range(feature):
                entry = 1 + feature + a * feature + b
                first[part, part * feature + a, entry] = 1.0
                second[part, part * feature + b, entry] = 1.0
    return first, second, add


def places():
    me = lax.axis_index("tok")
    core = me % 2
    x = (me // 2) % 2
    y = me // 4
    sib = me + 1 - 2 * core
    xn = me + 2 - 4 * x
    yn = me + 4 - 8 * y
    dg = xn + 4 - 8 * y
    return me, core, sib, (me, xn, yn, dg)


def enter(groups):
    me = lax.axis_index("tok")
    barrier = pltpu.get_barrier_semaphore()
    for step in range(1, 8):
        pl.semaphore_signal(
            barrier,
            inc=1,
            device_id={"tok": (me + step) % 8},
            device_id_type=pl.DeviceIdType.MESH,
        )
    for step in range(1, groups):
        pl.semaphore_signal(
            barrier,
            inc=1,
            device_id={"group": (lax.axis_index("group") + step) % groups},
            device_id_type=pl.DeviceIdType.MESH,
        )
    pl.semaphore_wait(barrier, 6 + groups)


def remote(src, dst, send, recv, target):
    return pltpu.make_async_remote_copy(
        src_ref=src,
        dst_ref=dst,
        send_sem=send,
        recv_sem=recv,
        device_id={"tok": target},
        device_id_type=pl.DeviceIdType.MESH,
    )


def block_at(ref, index, rows):
    return ref.at[pl.ds(pl.multiple_of(index * rows, rows), rows)]


def gather_rows(own_ref, all_ref, rows, send, recv, work):
    me, core, sib, peers = places()
    home = block_at(all_ref, me, rows)
    out = []
    for k in (1, 2, 3):
        copy = remote(own_ref, home, send.at[k], recv.at[k], peers[k])
        copy.start()
        out.append(copy)
    copy = remote(own_ref, home, send.at[4], recv.at[4], sib)
    copy.start()
    out.append(copy)
    home[...] = own_ref[...]

    def forward(k):
        landed = block_at(all_ref, peers[k], rows)
        remote(own_ref, landed, send.at[k], recv.at[k], peers[k]).wait_recv()
        copy = remote(landed, landed, send.at[4 + k], recv.at[4 + k], sib)
        copy.start()
        out.append(copy)

    def from_sibling(k):
        landed = block_at(all_ref, peers[k] + 1 - 2 * core, rows)
        remote(landed, landed, send.at[4 + k], recv.at[4 + k], sib).wait_recv()

    from_sibling(0)
    forward(1)
    from_sibling(1)
    work(me // 4)
    forward(2)
    forward(3)
    from_sibling(2)
    from_sibling(3)
    work(1 - me // 4)
    for copy in out:
        copy.wait_send()


def scatter_parts(part_ref, sib_ref, pair_ref, far_ref, rows, send, recv):
    me, core, sib, peers = places()
    near, far = {}, {}

    def emit(k):
        theirs = peers[k] + 1 - 2 * core
        copy = remote(block_at(part_ref, theirs, rows), sib_ref.at[k], send.at[k], recv.at[k], sib)
        copy.start()
        near[k] = copy

    def flush(k):
        near[k].wait_recv()
        pair_ref[k] = (
            block_at(part_ref, peers[k], rows)[...].astype(f32) + sib_ref[k].astype(f32)
        ).astype(bf16)
        copy = remote(pair_ref.at[k], far_ref.at[k], send.at[4 + k], recv.at[4 + k], peers[k])
        copy.start()
        far[k] = copy

    def finish():
        near[0].wait_recv()
        total = block_at(part_ref, me, rows)[...].astype(f32) + sib_ref[0].astype(f32)
        for k in (1, 2, 3):
            far[k].wait_recv()
            total = total + far_ref[k].astype(f32)
        for k in (0, 1, 2, 3):
            near[k].wait_send()
        for k in (1, 2, 3):
            far[k].wait_send()
        return total

    return emit, flush, finish


def pick_kernel(slot_ref, state_hbm, norm_ref, conv_ref, out_ref, held, load):
    phi_size, columns = state_hbm.shape[0], state_hbm.shape[2]
    head_count = norm_ref.shape[1]
    copies = []
    for i in range(8):
        copy = pltpu.make_async_copy(state_hbm.at[:, slot_ref[i], :], held.at[i], load.at[i])
        copy.start()
        copies.append(copy)
    first_head = slot_ref[8]
    row = lax.broadcasted_iota(jnp.int32, (head_count, wide), 0)
    col = lax.broadcasted_iota(jnp.int32, (head_count, wide), 1)
    choose = (
        (col >= columns) & (col < columns + 2) & (row == first_head + col - columns)
    ).astype(bf16)
    for i in range(8):
        slot = slot_ref[i]
        norms = lax.dot_general(
            norm_ref[slot].astype(bf16), choose, (((0,), (0,)), ((), ())), preferred_element_type=f32
        )
        out_ref[i, phi_size - 1 : slot_rows, :] = jnp.zeros((slot_rows - phi_size + 1, wide), bf16)
        out_ref[i, 0:phi_size, :] = norms.astype(bf16)
        out_ref[i, feat_rows : feat_rows + 2, 0:columns] = conv_ref[slot]
        copies[i].wait()
        out_ref[i, 0:phi_size, 0:columns] = held[i].astype(bf16)


def head_zero(shape, columns):
    col = lax.broadcasted_iota(jnp.int32, shape, 1)
    return (col < columns // 2) | (col == columns)


def local_kernel(
    groups,
    info_ref,
    own_ref,
    packed_ref,
    gain_ref,
    mixer_ref,
    qk_hbm,
    qk_out,
    v_out,
    conv_out,
    gate_out,
    acc_out,
    slots_out,
    rows_ref,
    normed,
    qk_ref,
    landed,
    send,
    recv,
    send_z,
    recv_z,
    load,
):
    rows = own_ref.shape[0]
    all_rows = rows_ref.shape[0]
    columns = mixer_ref.shape[1]
    feature = 16
    half = all_rows // 2
    me = lax.axis_index("tok")
    group_now = lax.axis_index("group")
    picked = pl.ds(pl.multiple_of(me * 2 * feature, 2 * feature), 2 * feature)
    qk_copy = pltpu.make_async_copy(qk_hbm.at[:, picked, :], qk_ref, load)
    qk_copy.start()
    enter(groups)
    shifts = []
    for step in range(1, groups):
        copy = pltpu.make_async_remote_copy(
            src_ref=packed_ref.at[pl.ds(2 * step, 2)],
            dst_ref=landed.at[step - 1],
            send_sem=send_z.at[step - 1],
            recv_sem=recv_z.at[step - 1],
            device_id={"group": (group_now + step) % groups},
            device_id_type=pl.DeviceIdType.MESH,
        )
        copy.start()
        shifts.append(copy)
    qk_copy.wait()

    def project(which):
        span = pl.ds(pl.multiple_of(which * half, half), half)
        x = rows_ref[span, :].astype(f32)
        scale = lax.rsqrt(jnp.mean(x * x, axis=-1, keepdims=True) + epsilon)
        normed[...] = (x * scale * gain_ref[0:1, :]).astype(bf16)
        v_out[span, :] = jnp.ones((half, wide), bf16)
        v_out[span, 0:columns] = dot_nt(normed[...], mixer_ref[0]).astype(bf16)
        conv_out[span, :] = dot_nt(normed[...], mixer_ref[1])
        gate_out[span, :] = dot_nt(normed[...], mixer_ref[2])
        qk_out[span, :] = dot_nt(normed[...], qk_ref[...].reshape(4 * feature, qk_ref.shape[2]))

    gather_rows(own_ref, rows_ref, rows, send, recv, project)

    block = 128

    @pl.loop(0, all_rows // block)
    def _(step):
        low = pl.multiple_of(step * block, block)
        span = pl.ds(low, block)
        query = qk_out[span, :]
        i = lax.broadcasted_iota(jnp.int32, (block, 1), 0) + low
        begin = jnp.zeros((block, 1), jnp.int32)
        for r in range(8):
            begin = jnp.where(i >= info_ref[r], info_ref[r], begin)
        j = lax.broadcasted_iota(jnp.int32, (block, all_rows), 1)
        allowed = (j <= i) & (j >= begin)
        found = []
        for h in range(2):
            q = query[:, h * feature : (h + 1) * feature].astype(bf16)
            k = qk_out[:, (2 + h) * feature : (3 + h) * feature].astype(bf16)
            s = dot_nt(q, k)
            w = jnp.where(allowed, 1.0 + 0.25 * s + s * s * (1.0 / 32.0), 0.0).astype(bf16)
            found.append(dot_nn(w, v_out[...]))
        acc_out[span, :] = jnp.where(head_zero((block, wide), columns), found[0], found[1])

    slots_out[0:2] = packed_ref[0:2]
    for step in range(1, groups):
        shifts[step - 1].wait()
        slots_out[2 * step : 2 * step + 2] = landed[step - 1]


def carried_kernel(
    info_ref,
    qk_ref,
    v_ref,
    conv_ref,
    gate_ref,
    acc_ref,
    slots_ref,
    first_ref,
    second_ref,
    add_ref,
    first_t_ref,
    second_t_ref,
    add_t_ref,
    taps_ref,
    att_out,
    gated_out,
    state_hbm,
    norm_out,
    cache_out,
    num,
    shifted,
    prev_one,
    prev_two,
    phi_q,
    phi_k,
    fresh_ref,
    store,
):
    all_rows, columns = conv_ref.shape
    phi_size = state_hbm.shape[0]
    norms = jnp.zeros((16, feat_rows), f32)
    norm_row = lax.broadcasted_iota(jnp.int32, (16, 128), 0)
    norm_col = lax.broadcasted_iota(jnp.int32, (16, 128), 1) - (columns - 128)
    pair = lax.broadcasted_iota(jnp.int32, (2, columns), 0)
    copies = []
    hi = qk_ref[...].astype(bf16)
    lo = (qk_ref[...] - hi.astype(f32)).astype(bf16)
    for h in range(2):
        one = dot_nn(hi, first_ref[h]) + dot_nn(lo, first_ref[h]) + add_ref[0:1]
        two = dot_nn(hi, second_ref[h]) + dot_nn(lo, second_ref[h]) + add_ref[1:2]
        phi_q[h] = (one * two * add_ref[2:3]).astype(bf16)
        one = dot_nt(first_t_ref[h], hi) + dot_nt(first_t_ref[h], lo) + add_t_ref[:, 0:1]
        two = dot_nt(second_t_ref[h], hi) + dot_nt(second_t_ref[h], lo) + add_t_ref[:, 1:2]
        phi_k[h] = (one * two * add_t_ref[:, 2:3]).astype(bf16)
    num[...] = acc_ref[...]
    shifted[0:8, :] = jnp.zeros((8, columns), f32)
    shifted[8 : 8 + all_rows, :] = conv_ref[...]
    prev_one[...] = shifted[7 : 7 + all_rows, :]
    prev_two[...] = shifted[6 : 6 + all_rows, :]
    i = lax.broadcasted_iota(jnp.int32, (all_rows, 1), 0)
    row_zero = head_zero((all_rows, wide), columns)
    state_zero = head_zero((feat_rows, wide), columns)
    for index in range(8):
        request = info_ref[24 + index]
        begin = info_ref[request]
        length = info_ref[8 + request]
        cached = info_ref[16 + request]
        end = begin + length
        live = jnp.where(cached > 0, 1.0, 0.0).astype(f32)
        state = slots_ref[index, 0:feat_rows, :]
        member = (i >= begin) & (i < end)
        carried = jnp.where(row_zero, dot_nn(phi_q[0], state), dot_nn(phi_q[1], state)) * live
        num[...] += jnp.where(member, carried, 0.0)
        mine = jnp.where(member, v_ref[...].astype(f32), 0.0).astype(bf16)
        added = jnp.where(state_zero, dot_nn(phi_k[0], mine), dot_nn(phi_k[1], mine))
        fresh = state.astype(f32) * live + added
        fresh_ref[index] = fresh[0:phi_size, 0:columns]
        copy = pltpu.make_async_copy(
            fresh_ref.at[index], state_hbm.at[:, request, :], store.at[index]
        )
        copy.start()
        copies.append(copy)
        choose = ((norm_row % 8 == request) & (norm_row // 8 == norm_col)).astype(bf16)
        norms = norms + dot_nt(choose, fresh[:, 128:256].astype(bf16))
        tail = slots_ref[index, feat_rows:slot_rows, 0:columns].astype(f32)
        newest = tail[1:2] * live
        oldest = tail[0:1] * jnp.where(cached >= 2, 1.0, 0.0).astype(f32)
        prev_one[...] = jnp.where(i == begin, newest, prev_one[...])
        prev_two[...] = jnp.where(
            i == begin, oldest, jnp.where((i == begin + 1) & (i < end), newest, prev_two[...])
        )
        final = shifted[pl.ds(7 + end, 1), :]
        before = shifted[pl.ds(6 + end, 1), :]
        before = jnp.where(length >= 2, before, newest)
        cache_out[request] = jnp.where(pair == 0, before, final).astype(bf16)
    col = lax.broadcasted_iota(jnp.int32, (all_rows, wide), 1)
    den = jnp.where(col < columns // 2, num[:, columns : columns + 1], num[:, columns + 1 : columns + 2])
    att_out[...] = (num[...] / den).astype(bf16)
    convolved = (
        taps_ref[0:1] * conv_ref[...] + taps_ref[1:2] * prev_one[...] + taps_ref[2:3] * prev_two[...]
    )
    gated_out[...] = (convolved * gate_ref[...]).astype(bf16)
    norm_out[...] = jnp.zeros(norm_out.shape, bf16)
    norm_out[:, 0:feat_rows] = norms.astype(bf16)
    for copy in copies:
        copy.wait()


def ffn_kernel(
    att_ref,
    gated_ref,
    weight_ref,
    own_ref,
    gain_ref,
    norm_ref,
    up_hbm,
    down_hbm,
    out_ref,
    norms_out,
    up,
    down,
    sib_a,
    pair_a,
    far_a,
    sib_b,
    pair_b,
    far_b,
    own_normed,
    normed,
    part_one,
    part_two,
    norms,
    send_a,
    recv_a,
    send_b,
    recv_b,
    send_g,
    recv_g,
    send_n,
    recv_n,
    load,
):
    rows = own_ref.shape[0]
    half = att_ref.shape[0] // 2
    columns = weight_ref.shape[1]
    up_copy = pltpu.make_async_copy(up_hbm, up, load.at[0])
    down_copy = pltpu.make_async_copy(down_hbm, down, load.at[1])
    up_copy.start()
    down_copy.start()
    enter(1)
    me = lax.axis_index("tok")

    def project(which):
        span = pl.ds(pl.multiple_of(which * half, half), half)
        part_one[span, :] = (
            dot_nn(att_ref[span, 0:columns], weight_ref[0])
            + dot_nn(gated_ref[span, :], weight_ref[1])
        ).astype(bf16)

    emit, flush, finish = scatter_parts(part_one, sib_a, pair_a, far_a, rows, send_a, recv_a)
    project(1 - me // 4)
    emit(3)
    emit(2)
    project(me // 4)
    emit(1)
    emit(0)
    for k in (3, 2, 1):
        flush(k)
    small = []
    for step in range(1, 8):
        copy = remote(
            norm_ref, norms.at[me], send_n.at[step - 1], recv_n.at[step - 1], (me + step) % 8
        )
        copy.start()
        small.append(copy)
    norms[me] = norm_ref[...]
    residual = own_ref[...].astype(f32) + finish()
    scale = lax.rsqrt(jnp.mean(residual * residual, axis=-1, keepdims=True) + epsilon)
    own_normed[...] = (residual * scale * gain_ref[1:2, :]).astype(bf16)
    up_copy.wait()
    down_copy.wait()
    emit, flush, finish = scatter_parts(part_two, sib_b, pair_b, far_b, rows, send_b, recv_b)

    def feed(which):
        span = pl.ds(pl.multiple_of(which * half, half), half)
        gate = dot_nt(normed[span, :], up[0])
        lift = dot_nt(normed[span, :], up[1])
        hidden = (gate / (1.0 + jnp.exp(-gate)) * lift).astype(bf16)
        part_two[span, :] = dot_nn(hidden, down[...]).astype(bf16)

    done = []

    def feed_and_send(which):
        feed(which)
        for k in (3, 2) if done else (1, 0):
            emit(k)
        for k in (3, 2) if done else (1,):
            flush(k)
        done.append(which)

    gather_rows(own_normed, normed, rows, send_g, recv_g, feed_and_send)
    out_ref[...] = (residual + finish()).astype(bf16)
    for step in range(1, 8):
        small[step - 1].wait_send()
        remote(
            norm_ref,
            norms.at[(me + 8 - step) % 8],
            send_n.at[step - 1],
            recv_n.at[step - 1],
            (me + step) % 8,
        ).wait_recv()
    norms_out[...] = norms[...]


def fast_device(
    tokens,
    norm_gains,
    qk_weight,
    mixer_weight,
    conv_weight,
    out_weight,
    ffn_weight,
    down_weight,
    cached_states,
    cached_norms,
    conv_cache,
    cached_lengths,
    new_lengths,
    state_source,
):
    rows, width = tokens.shape
    all_rows = 8 * rows
    requests, phi_size, columns = cached_states.shape
    head_count = cached_norms.shape[2]
    feature = qk_weight.shape[1] // head_count
    heads = 2
    groups = lax.axis_size("group")
    group_now = lax.axis_index("group")
    tok_now = lax.axis_index("tok")
    shape = jax.ShapeDtypeStruct
    dma = pltpu.SemaphoreType.DMA
    in_vmem = pl.BlockSpec(memory_space=VMEM)
    in_smem = pl.BlockSpec(memory_space=pltpu.SMEM)

    sources = state_source[:, 0].reshape(groups, requests)
    request = jnp.arange(requests, dtype=jnp.int32)
    shift = jnp.arange(groups, dtype=jnp.int32)

    def ends_of(match):
        low = jnp.min(jnp.where(match, request[None], requests - 1), axis=1)
        high = jnp.max(jnp.where(match, request[None], 0), axis=1)
        return jnp.stack([low, high], axis=1).reshape(-1).astype(jnp.int32)

    give = ends_of(sources[(group_now + shift) % groups] == group_now)
    own_sources = lax.dynamic_index_in_dim(sources, group_now, 0, keepdims=False)
    take = ends_of(own_sources[None] == ((group_now + groups - shift) % groups)[:, None])
    lengths = new_lengths[0]
    starts = jnp.cumsum(lengths) - lengths
    info = jnp.concatenate([starts, lengths, cached_lengths, take]).astype(jnp.int32)
    picks = jnp.concatenate([give, (tok_now * heads)[None].astype(jnp.int32)])

    in_any = pl.BlockSpec(memory_space=pl.ANY)
    packed = pl.pallas_call(
        pick_kernel,
        in_specs=[in_smem, in_any, in_vmem, in_vmem],
        out_specs=in_vmem,
        out_shape=shape((2 * groups, slot_rows, wide), bf16),
        scratch_shapes=[VMEM((8, phi_size, columns), f32), dma((8,))],
        compiler_params=pltpu.CompilerParams(vmem_limit_bytes=big_vmem),
        name="pick_slots",
    )(
        picks,
        jnp.transpose(cached_states, (1, 0, 2)),
        jnp.transpose(cached_norms, (0, 2, 1)),
        conv_cache,
    )

    qk, vext, conv_in, gate, acc, slots = pl.pallas_call(
        functools.partial(local_kernel, groups),
        in_specs=[in_smem, in_vmem, in_vmem, in_vmem, in_vmem, in_any],
        out_specs=[in_vmem] * 6,
        out_shape=[
            shape((all_rows, 4 * feature), f32),
            shape((all_rows, wide), bf16),
            shape((all_rows, columns), f32),
            shape((all_rows, columns), f32),
            shape((all_rows, wide), f32),
            shape((2 * groups, slot_rows, wide), bf16),
        ],
        scratch_shapes=[
            VMEM((all_rows, width), bf16),
            VMEM((all_rows // 2, width), bf16),
            VMEM((2, heads * feature, width), bf16),
            VMEM((groups - 1, 2, slot_rows, wide), bf16),
            dma((8,)),
            dma((8,)),
            dma((groups - 1,)),
            dma((groups - 1,)),
            dma,
        ],
        compiler_params=pltpu.CompilerParams(
            collective_id=0, has_side_effects=True, vmem_limit_bytes=big_vmem
        ),
        name="gather_and_local_attention",
    )(info, tokens, packed, norm_gains, mixer_weight, qk_weight)

    first, second, add = feature_tables(heads, feature)
    att, gated, new_states, share, cache_next = pl.pallas_call(
        carried_kernel,
        in_specs=[in_smem] + [in_vmem] * 13,
        out_specs=[in_vmem, in_vmem, in_any, in_vmem, in_vmem],
        out_shape=[
            shape((all_rows, wide), bf16),
            shape((all_rows, columns), bf16),
            shape((phi_size, requests, columns), f32),
            shape((heads * requests, 384), bf16),
            shape((requests, 2, columns), bf16),
        ],
        scratch_shapes=[
            VMEM((all_rows, wide), f32),
            VMEM((all_rows + 8, columns), f32),
            VMEM((all_rows, columns), f32),
            VMEM((all_rows, columns), f32),
            VMEM((2, all_rows, feat_rows), bf16),
            VMEM((2, feat_rows, all_rows), bf16),
            VMEM((8, phi_size, columns), f32),
            dma((8,)),
        ],
        compiler_params=pltpu.CompilerParams(vmem_limit_bytes=big_vmem),
        name="carried_states",
    )(
        info,
        qk,
        vext,
        conv_in,
        gate,
        acc,
        slots,
        jnp.asarray(first[:heads], bf16),
        jnp.asarray(second[:heads], bf16),
        jnp.asarray(add, f32),
        jnp.asarray(first[heads:].transpose(0, 2, 1), bf16),
        jnp.asarray(second[heads:].transpose(0, 2, 1), bf16),
        jnp.asarray(add.T, f32),
        conv_weight,
    )
    units = ffn_weight.shape[1]
    blocks = VMEM((4, rows, width), bf16)
    layer_out, norms = pl.pallas_call(
        ffn_kernel,
        in_specs=[in_vmem] * 6 + [in_any, in_any],
        out_specs=[in_vmem, in_vmem],
        out_shape=[shape((rows, width), bf16), shape((8,) + share.shape, bf16)],
        scratch_shapes=[
            VMEM((2, units, width), bf16),
            VMEM((units, width), bf16),
            blocks,
            blocks,
            blocks,
            blocks,
            blocks,
            blocks,
            VMEM((rows, width), bf16),
            VMEM((all_rows, width), bf16),
            VMEM((all_rows, width), bf16),
            VMEM((all_rows, width), bf16),
            VMEM((8,) + share.shape, bf16),
        ]
        + [dma((8,))] * 8
        + [dma((3,))],
        compiler_params=pltpu.CompilerParams(
            collective_id=1, has_side_effects=True, vmem_limit_bytes=big_vmem
        ),
        name="sum_and_ffn",
    )(att, gated, out_weight, tokens, norm_gains, share, ffn_weight, down_weight)
    norms = norms.reshape(8, heads, requests, -1)[:, :, :, :phi_size].astype(f32)
    new_norms = jnp.transpose(norms, (2, 3, 0, 1)).reshape(requests, phi_size, head_count)
    return (layer_out, jnp.transpose(new_states, (1, 0, 2)), new_norms, cache_next)


def device_function(mesh):
    if dict(mesh.shape) == {"group": 4, "tok": 8}:
        return fast_device
    return on_device


def solution(mesh):
    in_specs = (
        P(("group", "tok"), None),
        P(),
        P(),
        P(None, "tok", None),
        P(None, "tok"),
        P(None, "tok", None),
        P(None, "tok", None),
        P("tok", None),
        P("group", None, "tok"),
        P("group", None, None),
        P("group", None, "tok"),
        P("group"),
        P("group", None),
        P(),
    )
    out_specs = (
        P(("group", "tok"), None),
        P("group", None, "tok"),
        P("group", None, None),
        P("group", None, "tok"),
    )
    return jax.shard_map(
        device_function(mesh), mesh=mesh, in_specs=in_specs, out_specs=out_specs, check_vma=False
    )
```

```python
import functools
import math

import jax
import jax.numpy as jnp
import numpy as np
from jax import lax
from jax.experimental import pallas as pl
from jax.experimental.pallas import tpu as pltpu
from jax.sharding import PartitionSpec as P

epsilon = 1e-05
quad_scale = 0.25 / math.sqrt(2.0)
highest = lax.Precision.HIGHEST


def rms_scale(inputs, gain_row):
    widened = inputs.astype(jnp.float32)
    mean_sq = jnp.mean(widened * widened, axis=-1, keepdims=True)
    return widened * lax.rsqrt(mean_sq + epsilon) * gain_row


def taylor_features(vectors):
    row_count = vectors.shape[0]
    feat_count = vectors.shape[1]
    outer_terms = (vectors[:, :, None] * vectors[:, None, :]).reshape(
        row_count, feat_count * feat_count
    )
    return jnp.concatenate(
        [jnp.ones((row_count, 1), jnp.float32), 0.5 * vectors, quad_scale * outer_terms], axis=1
    )


def segment_layout(lengths, all_rows):
    request_ends = jnp.cumsum(lengths)
    request_starts = request_ends - lengths
    position = jnp.arange(all_rows, dtype=jnp.int32)
    segment = jnp.sum((position[:, None] >= request_ends[None, :]).astype(jnp.int32), axis=1)
    member = segment[:, None] == jnp.arange(lengths.shape[0], dtype=jnp.int32)[None, :]
    offset = position - jnp.sum(jnp.where(member, request_starts[None, :], 0), axis=1)
    return (request_ends, segment, member, offset)


def head_attention(
    queries, keys_head, values_head, state_head, norm_head, segment, member, query_block
):
    all_rows = queries.shape[0]
    requests, phi_size, value_width = state_head.shape
    state_flat = jnp.transpose(state_head, (1, 0, 2)).reshape(phi_size, requests * value_width)
    position = jnp.arange(all_rows, dtype=jnp.int32)
    pieces_out = []
    for first_row in range(0, all_rows, query_block):
        query_rows = queries[first_row : first_row + query_block]
        scores = lax.dot_general(query_rows, keys_head, (((1,), (1,)), ((), ())), precision=highest)
        kernel = 1.0 + 0.25 * scores + scores * scores / 32.0
        allowed = (segment[first_row : first_row + query_block, None] == segment[None, :]) & (
            position[None, :] <= position[first_row : first_row + query_block, None]
        )
        kernel = jnp.where(allowed, kernel, 0.0)
        local_den = jnp.sum(kernel, axis=1)
        local_num = jnp.dot(
            kernel.astype(jnp.bfloat16), values_head, preferred_element_type=jnp.float32
        )
        features = taylor_features(query_rows)
        carried = jnp.dot(features, state_flat, precision=highest).reshape(
            query_block, requests, value_width
        )
        owner = member[first_row : first_row + query_block]
        carried_num = jnp.sum(jnp.where(owner[:, :, None], carried, 0.0), axis=1)
        carried_den = jnp.sum(
            jnp.where(owner, jnp.dot(features, norm_head.T, precision=highest), 0.0), axis=1
        )
        pieces_out.append((local_num + carried_num) / (local_den + carried_den)[:, None])
    return jnp.concatenate(pieces_out, axis=0).astype(jnp.bfloat16)


def state_update(keys_head, values_head, member, state_head, norm_head):
    all_rows = keys_head.shape[0]
    requests, phi_size, value_width = state_head.shape
    features = taylor_features(keys_head)
    weights = member.astype(jnp.float32)
    spread = (weights[:, :, None] * values_head.astype(jnp.float32)[:, None, :]).reshape(
        all_rows, requests * value_width
    )
    added_state = lax.dot_general(features, spread, (((0,), (0,)), ((), ())), precision=highest)
    added_state = jnp.transpose(added_state.reshape(phi_size, requests, value_width), (1, 0, 2))
    norm_added = lax.dot_general(weights, features, (((0,), (0,)), ((), ())), precision=highest)
    return (state_head + added_state, norm_head + norm_added)


def short_conv(
    inputs, conv_gate, conv_taps, conv_state, cached_length, lengths, request_ends, member, offset
):
    all_rows = inputs.shape[0]
    channels = inputs.shape[1]
    cached = conv_state.astype(jnp.float32)
    last_cached = cached[:, 1] * (cached_length >= 1).astype(jnp.float32)[:, None]
    second_cached = cached[:, 0] * (cached_length >= 2).astype(jnp.float32)[:, None]
    last_rows = jnp.sum(jnp.where(member[:, :, None], last_cached[None], 0.0), axis=1)
    second_rows = jnp.sum(jnp.where(member[:, :, None], second_cached[None], 0.0), axis=1)
    shift_one = jnp.concatenate([jnp.zeros((1, channels), jnp.float32), inputs[:-1]], axis=0)
    shift_two = jnp.concatenate([jnp.zeros((2, channels), jnp.float32), inputs[:-2]], axis=0)
    within = offset[:, None]
    prev_one = jnp.where(within >= 1, shift_one, last_rows)
    prev_two = jnp.where(within >= 2, shift_two, jnp.where(within == 1, last_rows, second_rows))
    convolved = conv_taps[0] * inputs + conv_taps[1] * prev_one + conv_taps[2] * prev_two
    conv_out = (convolved * conv_gate).astype(jnp.bfloat16)
    position = jnp.arange(all_rows, dtype=jnp.int32)
    at_end = position[None, :] == (request_ends - 1)[:, None]
    before_end = position[None, :] == (request_ends - 2)[:, None]
    final_rows = jnp.sum(jnp.where(at_end[:, :, None], inputs[None], 0.0), axis=1)
    penultimate = jnp.sum(jnp.where(before_end[:, :, None], inputs[None], 0.0), axis=1)
    penultimate = jnp.where((lengths >= 2)[:, None], penultimate, last_cached)
    return (conv_out, jnp.stack([penultimate, final_rows], axis=1).astype(jnp.bfloat16))


def down_term(hidden, down_weight):
    return jnp.dot(hidden, down_weight, preferred_element_type=jnp.float32)


def on_device(
    tokens,
    norm_gains,
    qk_weight,
    mixer_weight,
    conv_weight,
    out_weight,
    ffn_weight,
    down_weight,
    cached_states,
    cached_norms,
    conv_cache,
    cached_lengths,
    new_lengths,
    state_source,
):
    tok_rows = tokens.shape[0]
    model_width = tokens.shape[1]
    shards = lax.axis_size("tok")
    requests = cached_states.shape[0]
    phi_size = cached_states.shape[1]
    columns = cached_states.shape[2]
    head_count = cached_norms.shape[2]
    head_width = model_width // head_count
    feature = qk_weight.shape[1] // head_count
    heads_here = max(1, columns // head_width)
    head_cols = columns // heads_here
    all_rows = tok_rows * shards
    query_block = math.gcd(all_rows, 512)
    group_now = lax.axis_index("group")
    tok_now = lax.axis_index("tok")
    first_head = tok_now * columns // head_width
    sources = state_source[:, 0]
    own_sources = lax.dynamic_slice_in_dim(sources, group_now * requests, requests)
    conv_wide = conv_cache.astype(jnp.float32)
    wanted = own_sources * requests + jnp.arange(requests, dtype=jnp.int32)
    blanks = (
        jnp.zeros_like(cached_states),
        jnp.zeros_like(cached_norms),
        jnp.zeros_like(conv_wide),
    )
    pieces = (
        lax.all_gather(cached_states.astype(jnp.bfloat16), "group", axis=0, tiled=True).astype(
            jnp.float32
        ),
        lax.all_gather(cached_norms.astype(jnp.bfloat16), "group", axis=0, tiled=True).astype(
            jnp.float32
        ),
        lax.all_gather(conv_wide.astype(jnp.bfloat16), "group", axis=0, tiled=True).astype(
            jnp.float32
        ),
    )
    row_count = pieces[0].shape[0]
    inside = (wanted >= 0) & (wanted < row_count)
    row_index = jnp.clip(wanted, 0, row_count - 1)
    fetched_states, fetched_norms, fetched_conv = tuple(
        (
            jnp.where(
                inside.reshape((requests,) + (1,) * (portion.ndim - 1)), portion[row_index], current
            )
            for portion, current in zip(pieces, blanks)
        )
    )
    has_state = (cached_lengths > 0).astype(jnp.float32)[:, None, None]
    start_states = fetched_states * has_state
    start_norms = fetched_norms * has_state
    qk_rows = lax.dynamic_slice_in_dim(
        qk_weight, first_head * feature, heads_here * feature, 1
    ).reshape(2 * heads_here * feature, model_width)
    in_rows = jnp.concatenate([mixer_weight.reshape(3 * columns, model_width), qk_rows], axis=0)
    whole_rows = lax.all_gather(tokens, "tok", axis=0, tiled=True)
    projected = lax.dot_general(
        rms_scale(whole_rows, norm_gains[0]).astype(jnp.bfloat16),
        in_rows,
        (((1,), (1,)), ((), ())),
        preferred_element_type=jnp.float32,
    )
    values = projected[:, :columns].astype(jnp.bfloat16)
    conv_in = projected[:, columns : 2 * columns]
    conv_gate = projected[:, 2 * columns : 3 * columns]
    lengths = new_lengths[0]
    request_ends, segment, member, offset = segment_layout(lengths, all_rows)
    pieces_out = []
    states_out = []
    norm_share = jnp.zeros((requests, phi_size, head_count), jnp.float32)
    for head_slot in range(heads_here):
        query_low = 3 * columns + head_slot * feature
        key_low = 3 * columns + (heads_here + head_slot) * feature
        queries = projected[:, query_low : query_low + feature]
        keys_head = projected[:, key_low : key_low + feature]
        values_head = values[:, head_slot * head_cols : (head_slot + 1) * head_cols]
        state_head = start_states[:, :, head_slot * head_cols : (head_slot + 1) * head_cols]
        norm_head = lax.dynamic_index_in_dim(start_norms, first_head + head_slot, 2, keepdims=False)
        pieces_out.append(
            head_attention(
                queries, keys_head, values_head, state_head, norm_head, segment, member, query_block
            )
        )
        state_next, norm_next = state_update(keys_head, values_head, member, state_head, norm_head)
        states_out.append(state_next)
        head_pick = (jnp.arange(head_count, dtype=jnp.int32) == first_head + head_slot).astype(
            jnp.float32
        )
        norm_share = norm_share + norm_next[:, :, None] * head_pick[None, None, :] * (
            head_cols / head_width
        )
    new_norms = lax.psum(norm_share.astype(jnp.bfloat16), "tok").astype(jnp.float32)
    conv_out, new_cache = short_conv(
        conv_in,
        conv_gate,
        conv_weight,
        fetched_conv,
        cached_lengths,
        lengths,
        request_ends,
        member,
        offset,
    )
    mixer_in = jnp.concatenate([jnp.concatenate(pieces_out, axis=1), conv_out], axis=1)
    out_rows = out_weight.reshape(2 * columns, model_width)
    ffn_units = ffn_weight.shape[1]
    ffn_rows_all = ffn_weight.reshape(2 * ffn_units, model_width)
    mixed_sum = lax.psum(
        jnp.dot(mixer_in, out_rows, preferred_element_type=jnp.float32).astype(jnp.bfloat16), "tok"
    ).astype(jnp.float32)
    residual = whole_rows.astype(jnp.float32) + mixed_sum
    both_parts = lax.dot_general(
        rms_scale(residual, norm_gains[1]).astype(jnp.bfloat16),
        ffn_rows_all,
        (((1,), (1,)), ((), ())),
        preferred_element_type=jnp.float32,
    )
    hidden = (jax.nn.silu(both_parts[:, :ffn_units]) * both_parts[:, ffn_units:]).astype(
        jnp.bfloat16
    )
    residual_own = lax.dynamic_slice_in_dim(residual, tok_now * tok_rows, tok_rows, 0)
    layer_out = (
        residual_own
        + lax.psum_scatter(
            down_term(hidden, down_weight).astype(jnp.bfloat16),
            "tok",
            scatter_dimension=0,
            tiled=True,
        ).astype(jnp.float32)
    ).astype(jnp.bfloat16)
    return (layer_out, jnp.concatenate(states_out, axis=2), new_norms, new_cache)


VMEM = pltpu.VMEM
wide = 256
feat_rows = 288
slot_rows = 304
big_vmem = 56 * 1024 * 1024
f32 = jnp.float32
bf16 = jnp.bfloat16


def dot_nt(left, right):
    return lax.dot_general(left, right, (((1,), (1,)), ((), ())), preferred_element_type=f32)


def dot_nn(left, right):
    return jnp.dot(left, right, preferred_element_type=f32)


def feature_tables(heads, feature):
    parts = 2 * heads
    first = np.zeros((parts, feature * parts, feat_rows), np.float32)
    second = np.zeros((parts, feature * parts, feat_rows), np.float32)
    add = np.zeros((3, feat_rows), np.float32)
    add[0, 0] = 1.0
    add[1, : 1 + feature] = 1.0
    add[2, 0] = 1.0
    add[2, 1 : 1 + feature] = 0.5
    add[2, 1 + feature : 1 + feature + feature * feature] = quad_scale
    for part in range(parts):
        for a in range(feature):
            first[part, part * feature + a, 1 + a] = 1.0
            for b in range(feature):
                entry = 1 + feature + a * feature + b
                first[part, part * feature + a, entry] = 1.0
                second[part, part * feature + b, entry] = 1.0
    return first, second, add


def places():
    me = lax.axis_index("tok")
    core = me % 2
    x = (me // 2) % 2
    y = me // 4
    sib = me + 1 - 2 * core
    xn = me + 2 - 4 * x
    yn = me + 4 - 8 * y
    dg = xn + 4 - 8 * y
    return me, core, sib, (me, xn, yn, dg)


def enter(groups):
    me = lax.axis_index("tok")
    barrier = pltpu.get_barrier_semaphore()
    for step in range(1, 8):
        pl.semaphore_signal(
            barrier,
            inc=1,
            device_id={"tok": (me + step) % 8},
            device_id_type=pl.DeviceIdType.MESH,
        )
    for step in range(1, groups):
        pl.semaphore_signal(
            barrier,
            inc=1,
            device_id={"group": (lax.axis_index("group") + step) % groups},
            device_id_type=pl.DeviceIdType.MESH,
        )
    pl.semaphore_wait(barrier, 6 + groups)


def remote(src, dst, send, recv, target):
    return pltpu.make_async_remote_copy(
        src_ref=src,
        dst_ref=dst,
        send_sem=send,
        recv_sem=recv,
        device_id={"tok": target},
        device_id_type=pl.DeviceIdType.MESH,
    )


def block_at(ref, index, rows):
    return ref.at[pl.ds(pl.multiple_of(index * rows, rows), rows)]


def gather_rows(own_ref, all_ref, rows, send, recv, work):
    me, core, sib, peers = places()
    home = block_at(all_ref, me, rows)
    out = []
    for k in (1, 2, 3):
        copy = remote(own_ref, home, send.at[k], recv.at[k], peers[k])
        copy.start()
        out.append(copy)
    copy = remote(own_ref, home, send.at[4], recv.at[4], sib)
    copy.start()
    out.append(copy)
    home[...] = own_ref[...]

    def forward(k):
        landed = block_at(all_ref, peers[k], rows)
        remote(own_ref, landed, send.at[k], recv.at[k], peers[k]).wait_recv()
        copy = remote(landed, landed, send.at[4 + k], recv.at[4 + k], sib)
        copy.start()
        out.append(copy)

    def from_sibling(k):
        landed = block_at(all_ref, peers[k] + 1 - 2 * core, rows)
        remote(landed, landed, send.at[4 + k], recv.at[4 + k], sib).wait_recv()

    forward(1)
    forward(2)
    from_sibling(0)
    from_sibling(1)
    work(me // 4)
    forward(3)
    from_sibling(2)
    from_sibling(3)
    work(1 - me // 4)
    for copy in out:
        copy.wait_send()


def scatter_parts(part_ref, sib_ref, pair_ref, far_ref, rows, send, recv):
    me, core, sib, peers = places()
    near, far = {}, {}

    def emit(k):
        theirs = peers[k] + 1 - 2 * core
        copy = remote(block_at(part_ref, theirs, rows), sib_ref.at[k], send.at[k], recv.at[k], sib)
        copy.start()
        near[k] = copy

    def flush(k):
        near[k].wait_recv()
        pair_ref[k] = (
            block_at(part_ref, peers[k], rows)[...].astype(f32) + sib_ref[k].astype(f32)
        ).astype(bf16)
        copy = remote(pair_ref.at[k], far_ref.at[k], send.at[4 + k], recv.at[4 + k], peers[k])
        copy.start()
        far[k] = copy

    def finish():
        near[0].wait_recv()
        total = block_at(part_ref, me, rows)[...].astype(f32) + sib_ref[0].astype(f32)
        for k in (1, 2, 3):
            far[k].wait_recv()
            total = total + far_ref[k].astype(f32)
        for k in (0, 1, 2, 3):
            near[k].wait_send()
        for k in (1, 2, 3):
            far[k].wait_send()
        return total

    return emit, flush, finish


def two_requests(source_ref, row_group, named):
    first, last = jnp.int32(7), jnp.int32(0)
    for r in range(8):
        last = jnp.where(source_ref[row_group * 8 + r] == named, r, last)
        first = jnp.where(source_ref[row_group * 8 + 7 - r] == named, 7 - r, first)
    return [first, last]


def pick_kernel(groups, source_ref, state_hbm, norm_ref, conv_ref, out_ref, held, load):
    phi_size, columns = state_hbm.shape[0], state_hbm.shape[2]
    head_count = norm_ref.shape[1]
    group_now = lax.axis_index("group")
    wanted = []
    for step in range(groups):
        wanted += two_requests(source_ref, (group_now + step) % groups, group_now)
    copies = []
    for i in range(8):
        copy = pltpu.make_async_copy(state_hbm.at[:, wanted[i], :], held.at[i], load.at[i])
        copy.start()
        copies.append(copy)
    first_head = lax.axis_index("tok") * 2
    row = lax.broadcasted_iota(jnp.int32, (head_count, wide), 0)
    col = lax.broadcasted_iota(jnp.int32, (head_count, wide), 1)
    choose = (
        (col >= columns) & (col < columns + 2) & (row == first_head + col - columns)
    ).astype(bf16)
    for i in range(8):
        slot = wanted[i]
        norms = lax.dot_general(
            norm_ref[slot].astype(bf16), choose, (((0,), (0,)), ((), ())), preferred_element_type=f32
        )
        out_ref[i, phi_size - 1 : slot_rows, :] = jnp.zeros((slot_rows - phi_size + 1, wide), bf16)
        out_ref[i, 0:phi_size, :] = norms.astype(bf16)
        out_ref[i, feat_rows : feat_rows + 2, 0:columns] = conv_ref[slot]
        copies[i].wait()
        out_ref[i, 0:phi_size, 0:columns] = held[i].astype(bf16)


def head_zero(shape, columns):
    col = lax.broadcasted_iota(jnp.int32, shape, 1)
    return (col < columns // 2) | (col == columns)


def local_kernel(
    groups,
    info_ref,
    own_ref,
    packed_ref,
    gain_ref,
    mixer_ref,
    qk_hbm,
    qk_out,
    v_out,
    conv_out,
    gate_out,
    acc_out,
    slots_out,
    rows_ref,
    normed,
    qk_ref,
    landed,
    send,
    recv,
    send_z,
    recv_z,
    load,
):
    rows = own_ref.shape[0]
    all_rows = rows_ref.shape[0]
    columns = mixer_ref.shape[1]
    feature = 16
    half = all_rows // 2
    me = lax.axis_index("tok")
    group_now = lax.axis_index("group")
    picked = pl.ds(pl.multiple_of(me * 2 * feature, 2 * feature), 2 * feature)
    qk_copy = pltpu.make_async_copy(qk_hbm.at[:, picked, :], qk_ref, load)
    qk_copy.start()
    enter(groups)
    shifts = []
    for step in range(1, groups):
        copy = pltpu.make_async_remote_copy(
            src_ref=packed_ref.at[pl.ds(2 * step, 2)],
            dst_ref=landed.at[step - 1],
            send_sem=send_z.at[step - 1],
            recv_sem=recv_z.at[step - 1],
            device_id={"group": (group_now + step) % groups},
            device_id_type=pl.DeviceIdType.MESH,
        )
        copy.start()
        shifts.append(copy)
    qk_copy.wait()

    def project(which):
        span = pl.ds(pl.multiple_of(which * half, half), half)
        x = rows_ref[span, :].astype(f32)
        scale = lax.rsqrt(jnp.mean(x * x, axis=-1, keepdims=True) + epsilon)
        normed[...] = (x * scale * gain_ref[0:1, :]).astype(bf16)
        v_out[span, :] = jnp.ones((half, wide), bf16)
        v_out[span, 0:columns] = dot_nt(normed[...], mixer_ref[0]).astype(bf16)
        conv_out[span, :] = dot_nt(normed[...], mixer_ref[1])
        gate_out[span, :] = dot_nt(normed[...], mixer_ref[2])
        qk_out[span, :] = dot_nt(normed[...], qk_ref[...].reshape(4 * feature, qk_ref.shape[2]))

    gather_rows(own_ref, rows_ref, rows, send, recv, project)

    block = 128

    @pl.loop(0, all_rows // block)
    def _(step):
        low = pl.multiple_of(step * block, block)
        span = pl.ds(low, block)
        query = qk_out[span, :]
        i = lax.broadcasted_iota(jnp.int32, (block, 1), 0) + low
        begin = jnp.zeros((block, 1), jnp.int32)
        start = jnp.int32(0)
        for r in range(8):
            begin = jnp.where(i >= start, start, begin)
            start = start + info_ref[0, r]
        j = lax.broadcasted_iota(jnp.int32, (block, all_rows), 1)
        allowed = (j <= i) & (j >= begin)
        found = []
        for h in range(2):
            q = query[:, h * feature : (h + 1) * feature].astype(bf16)
            k = qk_out[:, (2 + h) * feature : (3 + h) * feature].astype(bf16)
            s = dot_nt(q, k)
            w = jnp.where(allowed, 1.0 + 0.25 * s + s * s * (1.0 / 32.0), 0.0).astype(bf16)
            found.append(dot_nn(w, v_out[...]))
        acc_out[span, :] = jnp.where(head_zero((block, wide), columns), found[0], found[1])

    slots_out[0:2] = packed_ref[0:2]
    for step in range(1, groups):
        shifts[step - 1].wait()
        slots_out[2 * step : 2 * step + 2] = landed[step - 1]


def carried_kernel(
    groups,
    source_ref,
    lengths_ref,
    cached_ref,
    qk_ref,
    v_ref,
    conv_ref,
    gate_ref,
    acc_ref,
    slots_ref,
    first_ref,
    second_ref,
    add_ref,
    first_t_ref,
    second_t_ref,
    add_t_ref,
    taps_ref,
    att_out,
    gated_out,
    state_hbm,
    norm_out,
    cache_out,
    num,
    shifted,
    prev_one,
    prev_two,
    phi_q,
    phi_k,
    fresh_ref,
    store,
):
    all_rows, columns = conv_ref.shape
    phi_size = state_hbm.shape[0]
    norms = jnp.zeros((16, feat_rows), f32)
    norm_row = lax.broadcasted_iota(jnp.int32, (16, 128), 0)
    norm_col = lax.broadcasted_iota(jnp.int32, (16, 128), 1) - (columns - 128)
    pair = lax.broadcasted_iota(jnp.int32, (2, columns), 0)
    copies = []
    hi = qk_ref[...].astype(bf16)
    lo = (qk_ref[...] - hi.astype(f32)).astype(bf16)
    for h in range(2):
        one = dot_nn(hi, first_ref[h]) + dot_nn(lo, first_ref[h]) + add_ref[0:1]
        two = dot_nn(hi, second_ref[h]) + dot_nn(lo, second_ref[h]) + add_ref[1:2]
        phi_q[h] = (one * two * add_ref[2:3]).astype(bf16)
        one = dot_nt(first_t_ref[h], hi) + dot_nt(first_t_ref[h], lo) + add_t_ref[:, 0:1]
        two = dot_nt(second_t_ref[h], hi) + dot_nt(second_t_ref[h], lo) + add_t_ref[:, 1:2]
        phi_k[h] = (one * two * add_t_ref[:, 2:3]).astype(bf16)
    num[...] = acc_ref[...]
    shifted[0:8, :] = jnp.zeros((8, columns), f32)
    shifted[8 : 8 + all_rows, :] = conv_ref[...]
    prev_one[...] = shifted[7 : 7 + all_rows, :]
    prev_two[...] = shifted[6 : 6 + all_rows, :]
    i = lax.broadcasted_iota(jnp.int32, (all_rows, 1), 0)
    row_zero = head_zero((all_rows, wide), columns)
    state_zero = head_zero((feat_rows, wide), columns)
    group_now = lax.axis_index("group")
    taken = []
    for step in range(groups):
        taken += two_requests(source_ref, group_now, (group_now + groups - step) % groups)
    for index in range(8):
        request = taken[index]
        begin = jnp.int32(0)
        for r in range(7):
            begin = begin + jnp.where(r < request, lengths_ref[0, r], 0)
        length = lengths_ref[0, request]
        cached = cached_ref[request]
        end = begin + length
        live = jnp.where(cached > 0, 1.0, 0.0).astype(f32)
        state = slots_ref[index, 0:feat_rows, :]
        member = (i >= begin) & (i < end)
        carried = jnp.where(row_zero, dot_nn(phi_q[0], state), dot_nn(phi_q[1], state)) * live
        num[...] += jnp.where(member, carried, 0.0)
        mine = jnp.where(member, v_ref[...].astype(f32), 0.0).astype(bf16)
        added = jnp.where(state_zero, dot_nn(phi_k[0], mine), dot_nn(phi_k[1], mine))
        fresh = state.astype(f32) * live + added
        fresh_ref[index] = fresh[0:phi_size, 0:columns]
        copy = pltpu.make_async_copy(
            fresh_ref.at[index], state_hbm.at[:, request, :], store.at[index]
        )
        copy.start()
        copies.append(copy)
        choose = ((norm_row % 8 == request) & (norm_row // 8 == norm_col)).astype(bf16)
        norms = norms + dot_nt(choose, fresh[:, 128:256].astype(bf16))
        tail = slots_ref[index, feat_rows:slot_rows, 0:columns].astype(f32)
        newest = tail[1:2] * live
        oldest = tail[0:1] * jnp.where(cached >= 2, 1.0, 0.0).astype(f32)
        prev_one[...] = jnp.where(i == begin, newest, prev_one[...])
        prev_two[...] = jnp.where(
            i == begin, oldest, jnp.where((i == begin + 1) & (i < end), newest, prev_two[...])
        )
        final = shifted[pl.ds(7 + end, 1), :]
        before = shifted[pl.ds(6 + end, 1), :]
        before = jnp.where(length >= 2, before, newest)
        cache_out[request] = jnp.where(pair == 0, before, final).astype(bf16)
    col = lax.broadcasted_iota(jnp.int32, (all_rows, wide), 1)
    den = jnp.where(col < columns // 2, num[:, columns : columns + 1], num[:, columns + 1 : columns + 2])
    att_out[...] = (num[...] / den).astype(bf16)
    convolved = (
        taps_ref[0:1] * conv_ref[...] + taps_ref[1:2] * prev_one[...] + taps_ref[2:3] * prev_two[...]
    )
    gated_out[...] = (convolved * gate_ref[...]).astype(bf16)
    norm_out[...] = jnp.zeros(norm_out.shape, bf16)
    norm_out[:, 0:feat_rows] = norms.astype(bf16)
    for copy in copies:
        copy.wait()


def ffn_kernel(
    att_ref,
    gated_ref,
    weight_ref,
    own_ref,
    gain_ref,
    norm_ref,
    up_hbm,
    down_hbm,
    out_ref,
    norms_out,
    up,
    down,
    sib_a,
    pair_a,
    far_a,
    sib_b,
    pair_b,
    far_b,
    own_normed,
    normed,
    part_one,
    part_two,
    norms,
    send_a,
    recv_a,
    send_b,
    recv_b,
    send_g,
    recv_g,
    send_n,
    recv_n,
    load,
):
    rows = own_ref.shape[0]
    half = att_ref.shape[0] // 2
    columns = weight_ref.shape[1]
    up_copy = pltpu.make_async_copy(up_hbm, up, load.at[0])
    down_copy = pltpu.make_async_copy(down_hbm, down, load.at[1])
    up_copy.start()
    down_copy.start()
    enter(1)
    me = lax.axis_index("tok")

    def project(which):
        span = pl.ds(pl.multiple_of(which * half, half), half)
        part_one[span, :] = (
            dot_nn(att_ref[span, 0:columns], weight_ref[0])
            + dot_nn(gated_ref[span, :], weight_ref[1])
        ).astype(bf16)

    emit, flush, finish = scatter_parts(part_one, sib_a, pair_a, far_a, rows, send_a, recv_a)
    project(1 - me // 4)
    emit(3)
    emit(2)
    flush(3)
    flush(2)
    project(me // 4)
    emit(1)
    emit(0)
    flush(1)
    small = []
    for step in range(1, 8):
        copy = remote(
            norm_ref, norms.at[me], send_n.at[step - 1], recv_n.at[step - 1], (me + step) % 8
        )
        copy.start()
        small.append(copy)
    norms[me] = norm_ref[...]
    residual = own_ref[...].astype(f32) + finish()
    scale = lax.rsqrt(jnp.mean(residual * residual, axis=-1, keepdims=True) + epsilon)
    own_normed[...] = (residual * scale * gain_ref[1:2, :]).astype(bf16)
    up_copy.wait()
    down_copy.wait()
    emit, flush, finish = scatter_parts(part_two, sib_b, pair_b, far_b, rows, send_b, recv_b)

    def feed(which):
        span = pl.ds(pl.multiple_of(which * half, half), half)
        gate = dot_nt(normed[span, :], up[0])
        lift = dot_nt(normed[span, :], up[1])
        hidden = (gate / (1.0 + jnp.exp(-gate)) * lift).astype(bf16)
        part_two[span, :] = dot_nn(hidden, down[...]).astype(bf16)

    done = []

    def feed_and_send(which):
        if done:
            flush(1)
        feed(which)
        for k in (3, 2) if done else (1, 0):
            emit(k)
        if done:
            flush(3)
            flush(2)
        done.append(which)

    gather_rows(own_normed, normed, rows, send_g, recv_g, feed_and_send)
    out_ref[...] = (residual + finish()).astype(bf16)
    for step in range(1, 8):
        small[step - 1].wait_send()
        remote(
            norm_ref,
            norms.at[(me + 8 - step) % 8],
            send_n.at[step - 1],
            recv_n.at[step - 1],
            (me + step) % 8,
        ).wait_recv()
    norms_out[...] = norms[...]


def fast_device(
    tokens,
    norm_gains,
    qk_weight,
    mixer_weight,
    conv_weight,
    out_weight,
    ffn_weight,
    down_weight,
    cached_states,
    cached_norms,
    conv_cache,
    cached_lengths,
    new_lengths,
    state_source,
):
    rows, width = tokens.shape
    all_rows = 8 * rows
    requests, phi_size, columns = cached_states.shape
    head_count = cached_norms.shape[2]
    feature = qk_weight.shape[1] // head_count
    heads = 2
    groups = lax.axis_size("group")
    shape = jax.ShapeDtypeStruct
    dma = pltpu.SemaphoreType.DMA
    in_vmem = pl.BlockSpec(memory_space=VMEM)
    in_smem = pl.BlockSpec(memory_space=pltpu.SMEM)

    sources = state_source.reshape(-1)
    in_any = pl.BlockSpec(memory_space=pl.ANY)
    packed = pl.pallas_call(
        functools.partial(pick_kernel, groups),
        in_specs=[in_smem, in_any, in_vmem, in_vmem],
        out_specs=in_vmem,
        out_shape=shape((2 * groups, slot_rows, wide), bf16),
        scratch_shapes=[VMEM((8, phi_size, columns), f32), dma((8,))],
        compiler_params=pltpu.CompilerParams(vmem_limit_bytes=big_vmem),
        name="pick_slots",
    )(
        sources,
        jnp.transpose(cached_states, (1, 0, 2)),
        jnp.transpose(cached_norms, (0, 2, 1)),
        conv_cache,
    )

    qk, vext, conv_in, gate, acc, slots = pl.pallas_call(
        functools.partial(local_kernel, groups),
        in_specs=[in_smem, in_vmem, in_vmem, in_vmem, in_vmem, in_any],
        out_specs=[in_vmem] * 6,
        out_shape=[
            shape((all_rows, 4 * feature), f32),
            shape((all_rows, wide), bf16),
            shape((all_rows, columns), f32),
            shape((all_rows, columns), f32),
            shape((all_rows, wide), f32),
            shape((2 * groups, slot_rows, wide), bf16),
        ],
        scratch_shapes=[
            VMEM((all_rows, width), bf16),
            VMEM((all_rows // 2, width), bf16),
            VMEM((2, heads * feature, width), bf16),
            VMEM((groups - 1, 2, slot_rows, wide), bf16),
            dma((8,)),
            dma((8,)),
            dma((groups - 1,)),
            dma((groups - 1,)),
            dma,
        ],
        compiler_params=pltpu.CompilerParams(
            collective_id=0, has_side_effects=True, vmem_limit_bytes=big_vmem
        ),
        name="gather_and_local_attention",
    )(new_lengths, tokens, packed, norm_gains, mixer_weight, qk_weight)

    first, second, add = feature_tables(heads, feature)
    att, gated, new_states, share, cache_next = pl.pallas_call(
        functools.partial(carried_kernel, groups),
        in_specs=[in_smem] * 3 + [in_vmem] * 13,
        out_specs=[in_vmem, in_vmem, in_any, in_vmem, in_vmem],
        out_shape=[
            shape((all_rows, wide), bf16),
            shape((all_rows, columns), bf16),
            shape((phi_size, requests, columns), f32),
            shape((heads * requests, 384), bf16),
            shape((requests, 2, columns), bf16),
        ],
        scratch_shapes=[
            VMEM((all_rows, wide), f32),
            VMEM((all_rows + 8, columns), f32),
            VMEM((all_rows, columns), f32),
            VMEM((all_rows, columns), f32),
            VMEM((2, all_rows, feat_rows), bf16),
            VMEM((2, feat_rows, all_rows), bf16),
            VMEM((8, phi_size, columns), f32),
            dma((8,)),
        ],
        compiler_params=pltpu.CompilerParams(vmem_limit_bytes=big_vmem),
        name="carried_states",
    )(
        sources,
        new_lengths,
        cached_lengths,
        qk,
        vext,
        conv_in,
        gate,
        acc,
        slots,
        jnp.asarray(first[:heads], bf16),
        jnp.asarray(second[:heads], bf16),
        jnp.asarray(add, f32),
        jnp.asarray(first[heads:].transpose(0, 2, 1), bf16),
        jnp.asarray(second[heads:].transpose(0, 2, 1), bf16),
        jnp.asarray(add.T, f32),
        conv_weight,
    )
    units = ffn_weight.shape[1]
    blocks = VMEM((4, rows, width), bf16)
    layer_out, norms = pl.pallas_call(
        ffn_kernel,
        in_specs=[in_vmem] * 6 + [in_any, in_any],
        out_specs=[in_vmem, in_vmem],
        out_shape=[shape((rows, width), bf16), shape((8,) + share.shape, bf16)],
        scratch_shapes=[
            VMEM((2, units, width), bf16),
            VMEM((units, width), bf16),
            blocks,
            blocks,
            blocks,
            blocks,
            blocks,
            blocks,
            VMEM((rows, width), bf16),
            VMEM((all_rows, width), bf16),
            VMEM((all_rows, width), bf16),
            VMEM((all_rows, width), bf16),
            VMEM((8,) + share.shape, bf16),
        ]
        + [dma((8,))] * 8
        + [dma((3,))],
        compiler_params=pltpu.CompilerParams(
            collective_id=1, has_side_effects=True, vmem_limit_bytes=big_vmem
        ),
        name="sum_and_ffn",
    )(att, gated, out_weight, tokens, norm_gains, share, ffn_weight, down_weight)
    norms = norms.reshape(8, heads, requests, -1)[:, :, :, :phi_size].astype(f32)
    new_norms = jnp.transpose(norms, (2, 3, 0, 1)).reshape(requests, phi_size, head_count)
    return (layer_out, jnp.transpose(new_states, (1, 0, 2)), new_norms, cache_next)


def device_function(mesh):
    if dict(mesh.shape) == {"group": 4, "tok": 8}:
        return fast_device
    return on_device


def solution(mesh):
    in_specs = (
        P(("group", "tok"), None),
        P(),
        P(),
        P(None, "tok", None),
        P(None, "tok"),
        P(None, "tok", None),
        P(None, "tok", None),
        P("tok", None),
        P("group", None, "tok"),
        P("group", None, None),
        P("group", None, "tok"),
        P("group"),
        P("group", None),
        P(),
    )
    out_specs = (
        P(("group", "tok"), None),
        P("group", None, "tok"),
        P("group", None, None),
        P("group", None, "tok"),
    )
    return jax.shard_map(
        device_function(mesh), mesh=mesh, in_specs=in_specs, out_specs=out_specs, check_vma=False
    )
```
